256 devices in a mesh: section: 2 (over core), tensor: 16 (over y, x), dp: 8 (over z).
Axes of the slice: x: 4, y: 4, z: 8, core: 2. Of those that a mesh axis runs over, the one named last changes fastest.
Arguments:
- hidden_in: bfloat16 [8, 256, 6144], P('dp', None, 'tensor'), may hold values from -45 to 45
- doc_lengths: int32 [8, 4], P('dp'), may hold values from 1 to 128, 256 in all within a row
- w_qkv: bfloat16 [2, 6144, 18432], P('section', 'dp', 'tensor'), may hold values from -4 to 4
- w_out: bfloat16 [2, 6144, 6144], P('section', 'dp', 'tensor'), may hold values from -0.078125 to 0.078125
Outputs:
- layer_states: bfloat16 [2, 8, 256, 6144], P('section', 'dp', None, 'tensor')
The draws below stay inside these ranges and needn't reach their ends.
Inputs may be any that keep to these rules, and one draw needn't show every extreme that they name: `doc_lengths`: each row gives the lengths of 4 packed documents in order, summing to 256.
All inputs are finite; a program needn't handle non-finite values.
Results may differ from the reference program's by a relative error of at most 0.0041.
Values may be sent and summed in bfloat16 or wider, within the bound.
A program may use at most 64 MiB of HBM per device.

```python
import math
import jax
import jax.numpy as jnp
import numpy as np
from jax import lax

D = 6144
HD = 128
HEADS = 48
LEN = 256
SEQS = 8
DOCS = 4
LAYERS = 2


def draw_hidden_in(key, part):
    key = jax.random.fold_in(key, 11)
    noise_key, scale_key = jax.random.split(key, 2)
    row_scale = jnp.exp(jax.random.uniform(scale_key, (SEQS, LEN, 1), jnp.float32, 0.0, math.log(10.0)))
    base = jnp.clip(jax.random.normal(noise_key, (SEQS, LEN, D), jnp.float32), -4.0, 4.0)
    values_all = base * row_scale
    return values_all.astype(jnp.bfloat16)


def draw_w_qkv(key, part):
    key = jax.random.fold_in(key, 23)
    query_key, keys_key, value_key = jax.random.split(key, 3)
    full_shape = (LAYERS, D, HEADS, HD)
    root_width = math.sqrt(D)
    query_part = jnp.clip(jax.random.normal(query_key, full_shape, jnp.float32), -4.0, 4.0)
    key_noise = jnp.clip(jax.random.normal(keys_key, full_shape, jnp.float32), -4.0, 4.0)
    value_part = jnp.clip(jax.random.normal(value_key, full_shape, jnp.float32), -4.0, 4.0) / root_width
    query_part = query_part / root_width
    key_part = key_noise / root_width
    stacked = jnp.stack([query_part, key_part, value_part], axis=3)
    return stacked.reshape(LAYERS, D, 3 * HEADS * HD).astype(jnp.bfloat16)


def block_levels(own_key, extent, shards, low, largest):
    def one(dim, blocks):
        steps = jax.random.uniform(jax.random.fold_in(jax.random.fold_in(own_key, 6), dim), (blocks,), jnp.float32, low / len(shards), largest / len(shards))
        return jnp.repeat(jnp.exp(steps), extent[dim] // blocks).reshape((-1,) + (1,) * (len(extent) - dim - 1))

    level = one(*shards[0])
    for cut in shards[1:]:
        level = level * one(*cut)
    return level


def profile(count, total, limit, lean):
    weights = [(1 << 20) // math.isqrt(rank ** lean) + 1 for rank in range(2, count + 1)]
    spare, given = total - limit - (count - 1), [1] * (count - 1)
    while spare > 0:
        free = [i for i in range(count - 1) if given[i] < limit]
        pool, left = sum([weights[i] for i in free]), spare
        for i in free:
            extra = min(limit - given[i], max(1, left * weights[i] // pool), spare)
            given[i] = given[i] + extra
            spare = spare - extra
    return np.array([limit] + given)


def ragged_sizes(key, count, total, reach, slope):
    if count == 2:
        one = jax.random.randint(key, (), max(1, total - reach), min(reach, total - 1) + 1)
        return jnp.stack([one, total - one])
    sizes = jnp.asarray(profile(count, total, reach, slope), jnp.int32)
    couples = (count - 1) // 2
    source_of, receiver = sizes[1:1 + 2 * couples:2], sizes[2:2 + 2 * couples:2]
    room = jnp.minimum(source_of - 1, reach - receiver)
    passed = jax.random.randint(jax.random.fold_in(key, 1), (couples,), 0, 1 << 20) % (room + 1)
    sizes = sizes.at[1:1 + 2 * couples:2].set(source_of - passed).at[2:2 + 2 * couples:2].set(receiver + passed)
    return sizes[jax.random.permutation(jax.random.fold_in(key, 2), count)]


def normal_values(rng, extent, width, limit, pieces=(), held_as=jnp.bfloat16):
    entries = width * jax.random.normal(rng, extent, jnp.float32)
    if pieces:
        entries = entries * block_levels(rng, extent, pieces, -0.22, 0.18)
    return jnp.clip(entries, -limit, limit).astype(held_as)


def setup_inputs(seed: int = 0) -> dict:
    streams_of = jax.random.split(jax.random.key(seed), 5)
    return {
        "hidden_in": draw_hidden_in(jax.random.fold_in(streams_of[4], 71), 0),
        "doc_lengths": jax.vmap(lambda own: ragged_sizes(own, DOCS, LEN, LEN // 2, 2))(jax.random.split(streams_of[1], SEQS)).reshape((SEQS, DOCS)).astype(jnp.int32),
        "w_qkv": draw_w_qkv(jax.random.fold_in(streams_of[4], 71), 0),
        "w_out": normal_values(streams_of[3], (LAYERS, HEADS * HD, D), (HEADS * HD) ** -0.5, 0.078125, ((0, 2), (1, 8), (2, 16))),
    }


def normalize(values_rows):
    average = lax.optimization_barrier(jnp.mean(values_rows, axis=-1, keepdims=True))
    centred = values_rows - average
    spread = lax.optimization_barrier(jnp.mean(centred * centred, axis=-1, keepdims=True))
    return centred * lax.rsqrt(spread + 1e-05)

def reference(hidden_in, doc_lengths, w_qkv, w_out):
    positions = jnp.arange(LEN, dtype=jnp.int32)
    score_scale = 1.0 / math.sqrt(HD)

    def one_sequence(operands):
        stream, lengths = operands
        doc_ends = jnp.cumsum(lengths).astype(jnp.int32)
        doc_of = lax.optimization_barrier(jnp.sum((positions[:, None] >= doc_ends[None, :]).astype(jnp.int32), axis=1))
        allowed = (positions[None, :] <= positions[:, None]) & (doc_of[None, :] == doc_of[:, None])

        def apply_layer(stream, weights):
            qkv_weight, out_weight = weights
            normed = normalize(stream.astype(jnp.float32)).astype(jnp.bfloat16)
            projected = jnp.dot(normed, qkv_weight, preferred_element_type=jnp.float32)
            projected = projected.astype(jnp.bfloat16).reshape(LEN, HEADS, 3, HD).astype(jnp.float32)
            scores = jnp.einsum('qhd,khd->hqk', projected[:, :, 0], projected[:, :, 1]) * score_scale
            scores = jnp.where(allowed[None], scores, -1e+30)
            row_max = lax.optimization_barrier(jnp.max(scores, axis=-1, keepdims=True))
            weights_exp = jnp.exp(scores - row_max)
            softmax_out = (weights_exp / lax.optimization_barrier(jnp.sum(weights_exp, axis=-1, keepdims=True))).astype(jnp.bfloat16)
            attended = jnp.einsum('hqk,khd->qhd', softmax_out.astype(jnp.float32), projected[:, :, 2])
            attended = attended.astype(jnp.bfloat16).reshape(LEN, HEADS * HD)
            update = jnp.dot(attended, out_weight, preferred_element_type=jnp.float32)
            result = (stream.astype(jnp.float32) + update).astype(jnp.bfloat16)
            return (result, result)
        final_state, states = lax.scan(apply_layer, stream, (w_qkv, w_out))
        return states
    per_sequence = lax.map(one_sequence, (hidden_in, doc_lengths))
    return jnp.transpose(per_sequence, (1, 0, 2, 3))
```

```python
import functools
import math

import jax
import jax.numpy as jnp
from jax import lax
from jax.experimental import pallas as pl
from jax.experimental.pallas import tpu as pltpu
from jax.sharding import PartitionSpec as P

MESH = pl.DeviceIdType.MESH
HD = 128
HEADS = 3
LEN = 256
FEAT = 384
ROWS = 768
COLS = 1152
WIDTH = 6144
NZ = 8
GROUPS = ((0, 1), (1, 2), (3, 2), (5, 2), (7, 1))
F32 = jnp.float32
BF16 = jnp.bfloat16


def kernel(
    doc_ref, hid_ref, wq_hbm, wo_hbm, out_ref,
    xin, xc, wq, wo, stat, csum, trans, mask, proj, att, res,
    xbuf, abuf, part, send3, recv3, part6, send6, recv6,
    load_sem, hand_sem,
    s1s, s1r, s4s, s4r, a2s, a2r, b2s, b2r, a5s, a5r, b5s, b5r,
    sts, str_, css, csr, s3s, s3r, s6s, s6r,
):
    s = lax.axis_index("section")
    t = lax.axis_index("tensor")
    z = lax.axis_index("dp")
    y, x = t // 4, t % 4
    plane = t // 2
    half = t % 2
    at_home = plane == z

    def along_z(by):
        return (s, t, (z + by + NZ) % NZ)

    def in_plane(dy, dx):
        return (s, ((y + dy) % 4) * 4 + (x + dx) % 4, z)

    def copy(src, dst, send_sem, recv_sem, device):
        return pltpu.make_async_remote_copy(
            src_ref=src, dst_ref=dst, send_sem=send_sem, recv_sem=recv_sem,
            device_id=device, device_id_type=MESH,
        )

    load_q = pltpu.make_async_copy(wq_hbm.at[0], wq, load_sem.at[0])
    load_o = pltpu.make_async_copy(wo_hbm.at[0], wo, load_sem.at[1])
    load_x = pltpu.make_async_copy(hid_ref.at[0], xin, load_sem.at[2])

    @pl.when(s == 0)
    def _():
        load_x.start()

    load_q.start()
    load_o.start()

    barrier = pltpu.get_barrier_semaphore()

    def greet(device):
        pl.semaphore_signal(barrier, inc=1, device_id=device, device_id_type=MESH)

    def greet_source(i, c):
        source_t, source_z = 2 * z + i % 2, i // 2

        @pl.when(jnp.logical_not((source_t == t) & (source_z == z)))
        def _():
            greet((s, source_t, source_z))

        return c

    lax.fori_loop(0, 16, greet_source, 0)

    def greet_plane(i, c):
        greet(in_plane(i // 4, i % 4))
        return c

    lax.fori_loop(1, 16, greet_plane, 0)

    def greet_line(i, c):
        greet(along_z(i))
        return c

    lax.fori_loop(1, NZ, greet_line, 0)
    greet((1 - s, t, z))
    pl.semaphore_wait(barrier, 16 + 15 + 7 + 1 - at_home.astype(jnp.int32))

    hand = copy(res, xin, hand_sem.at[0], hand_sem.at[1], (1 - s, t, z))

    @pl.when(s == 0)
    def _():
        load_x.wait()

    @pl.when(s == 1)
    def _():
        hand.wait_recv()

    xf = xin[...].astype(F32)
    own_mean = jnp.mean(xf, axis=1, keepdims=True)
    centred = xf - own_mean
    own_sq = jnp.sum(centred * centred, axis=1, keepdims=True)
    xc[...] = centred.astype(BF16)

    rel = (z - plane + NZ) % NZ
    slot = jnp.where(rel < 4, 7 - 2 * rel, 2 * rel - 8)

    def spread_copy(src, buf, ssem, rsem, g):
        rows = pl.ds(pl.multiple_of(g * 16, 16), 16)
        there = pl.ds(pl.multiple_of((g % 4) * 16, 16), 16)
        cols = pl.ds(pl.multiple_of(half * FEAT, 128), FEAT)
        from_ref, to_ref = src.at[rows, :], buf.at[slot, g // 4, there, cols]

        def remote():
            return copy(from_ref, to_ref, ssem.at[g], rsem.at[slot, half], (s, g, plane))

        def local():
            return pltpu.make_async_copy(from_ref, to_ref, rsem.at[slot, half])

        return remote, local

    def spread(src, buf, ssem, rsem):
        def body(g, c):
            remote, local = spread_copy(src, buf, ssem, rsem, g)
            own = at_home & (g == t)

            @pl.when(own)
            def _():
                local().start()

            @pl.when(jnp.logical_not(own))
            def _():
                remote().start()

            return c

        lax.fori_loop(0, 16, body, 0)

    def spread_drain(src, buf, ssem, rsem):
        def body(g, c):
            remote, _ = spread_copy(src, buf, ssem, rsem, g)

            @pl.when(jnp.logical_not(at_home & (g == t)))
            def _():
                remote().wait_send()

            return c

        lax.fori_loop(0, 16, body, 0)

    def spread_wait(buf, rsem, k, h):
        there = buf.at[k, y, pl.ds(pl.multiple_of(x * 16, 16), 16), pl.ds(h * FEAT, FEAT)]
        pltpu.make_async_copy(there, there, rsem.at[k, h]).wait()

    def gather_copy(buf, sems, step, grp, h, j):
        k0, n = GROUPS[grp]
        own = pl.ds(pl.multiple_of(x * 16, 16), 16)
        cols = pl.ds(h * FEAT, FEAT)
        if step == 0:
            ref = buf.at[pl.ds(k0, n), y, own, cols]
        elif h == 0:
            ref = buf.at[pl.ds(k0, n), y, :, cols]
        else:
            ref = buf.at[pl.ds(k0, n), :, own, cols]
        device = in_plane(0, j) if (step == h) else in_plane(j, 0)
        return copy(ref, ref, sems[2 * step].at[grp, h, j - 1], sems[2 * step + 1].at[grp, h, j - 1], device)

    def gather_first(buf, sems, rsem, grp):
        k0, n = GROUPS[grp]
        for h in range(2):
            for k in range(k0, k0 + n):
                spread_wait(buf, rsem, k, h)
            for j in (2, 1, 3):
                gather_copy(buf, sems, 0, grp, h, j).start()

    def gather_second(buf, sems, grp):
        for h in range(2):
            for j in (1, 2, 3):
                gather_copy(buf, sems, 0, grp, h, j).wait_recv()
            for j in (2, 1, 3):
                gather_copy(buf, sems, 1, grp, h, j).start()

    def gather_last(buf, sems, grp):
        for h in range(2):
            for j in (1, 2, 3):
                gather_copy(buf, sems, 1, grp, h, j).wait_recv()

    def gather_drain(buf, sems):
        for grp in range(len(GROUPS)):
            for step in range(2):
                for h in range(2):
                    for j in (1, 2, 3):
                        gather_copy(buf, sems, step, grp, h, j).wait_send()

    spread(xc, xbuf, s1s, s1r)

    lane = lax.broadcasted_iota(jnp.int32, (LEN, 128), 1)
    columns = jnp.where(lane == 0, own_mean, jnp.where(lane == 1, own_sq, 0.0))
    stat[t] = jnp.transpose(columns)[0:8, :]

    def stat_copy(i):
        return copy(stat.at[t], stat.at[t], sts.at[i - 1], str_.at[i - 1], in_plane(i // 4, i % 4))

    def stat_send(i, c):
        stat_copy(i).start()
        return c

    lax.fori_loop(1, 16, stat_send, 0)

    load_q.wait()
    row16 = lax.broadcasted_iota(jnp.int32, (16, ROWS), 0)
    col16 = lax.broadcasted_iota(jnp.int32, (16, ROWS), 1)
    pick = jnp.where(row16 == col16 // FEAT, 1.0, 0.0).astype(BF16)
    csum[z] = jnp.dot(pick, wq[...], preferred_element_type=F32)[0:8, :]
    csum[NZ : 2 * NZ] = jnp.zeros((NZ, 8, COLS), F32)

    def csum_copy(i):
        return copy(csum.at[z], csum.at[z], css.at[i - 1], csr.at[i - 1], along_z(i))

    def csum_send(i, c):
        csum_copy(i).start()
        return c

    lax.fori_loop(1, NZ, csum_send, 0)

    sems2 = (a2s, a2r, b2s, b2r)
    sems5 = (a5s, a5r, b5s, b5r)

    def product(buf, k, w, into, tiles):
        rows = buf[k].reshape(LEN, ROWS)

        def body(n, c):
            cols = pl.ds(pl.multiple_of(n * FEAT, 128), FEAT)
            into[k, :, cols] = jnp.dot(rows, w[:, cols], preferred_element_type=F32)
            return c

        lax.fori_loop(0, tiles, body, 0)

    def ring_copy(k, q):
        rows = pl.ds(q * 64, 64)
        up = q < 2 if k == 0 else k % 2 == 1
        return copy(send3.at[k, rows], recv3.at[k, rows], s3s.at[k, q], s3r.at[k, q], along_z(1 if up else -1))

    def ring_step(k, q, before):
        rows = pl.ds(q * 64, 64)
        value = part[k, rows, :]
        if before is not None:
            ring_copy(before, q).wait_recv()
            value = value + recv3[before, rows, :].astype(F32)
        send3[k, rows, :] = value.astype(BF16)
        ring_copy(k, q).start()

    for grp in range(5):
        gather_first(xbuf, sems2, s1r, grp)

    row_pos = lax.broadcasted_iota(jnp.int32, (LEN, LEN), 0)
    col_pos = lax.broadcasted_iota(jnp.int32, (LEN, LEN), 1)
    row_doc = jnp.zeros((LEN, LEN), jnp.int32)
    col_doc = jnp.zeros((LEN, LEN), jnp.int32)
    end = jnp.int32(0)
    for i in range(4):
        end = end + doc_ref[0, i]
        row_doc = row_doc + (row_pos >= end).astype(jnp.int32)
        col_doc = col_doc + (col_pos >= end).astype(jnp.int32)
    mask[...] = jnp.where((col_pos <= row_pos) & (row_doc == col_doc), 1.0, 0.0)

    gather_second(xbuf, sems2, 0)
    gather_second(xbuf, sems2, 1)
    gather_last(xbuf, sems2, 0)
    product(xbuf, 0, wq, part, 3)
    for q in (0, 2, 1, 3):
        ring_step(0, q, None)
    gather_second(xbuf, sems2, 2)
    gather_last(xbuf, sems2, 1)
    product(xbuf, 1, wq, part, 3)
    ring_step(1, 2, None)
    ring_step(1, 3, None)
    product(xbuf, 2, wq, part, 3)
    ring_step(2, 0, None)
    ring_step(2, 1, None)
    gather_second(xbuf, sems2, 3)
    gather_last(xbuf, sems2, 2)
    product(xbuf, 3, wq, part, 3)
    product(xbuf, 4, wq, part, 3)
    ring_step(1, 0, 0)
    ring_step(2, 2, 0)
    ring_step(1, 1, 0)
    ring_step(2, 3, 0)
    gather_second(xbuf, sems2, 4)
    gather_last(xbuf, sems2, 3)
    product(xbuf, 5, wq, part, 3)
    product(xbuf, 6, wq, part, 3)
    up_order, down_order = (2, 3, 0, 1), (0, 1, 2, 3)
    for i in range(4):
        ring_step(3, up_order[i], 1)
        ring_step(4, down_order[i], 2)
    gather_last(xbuf, sems2, 4)
    product(xbuf, 7, wq, part, 3)
    for i in range(4):
        ring_step(5, up_order[i], 3)
        ring_step(6, down_order[i], 4)

    for i in range(1, 16):
        stat_copy(i).wait_recv()
    means = [stat[i, 0:1, :] for i in range(16)]
    mean = functools.reduce(lambda a, b: a + b, means) * (1.0 / 16)
    square = functools.reduce(lambda a, b: a + b, [stat[i, 1:2, :] for i in range(16)])
    trans[...] = jnp.zeros((128, LEN), F32)
    for i in range(16):
        off = means[i] - mean
        square = square + FEAT * (off * off)
        trans[pl.ds((i // 2) * 8 + i % 2, 1), :] = off
    trans[pl.ds(64, 1), :] = lax.rsqrt(square * (1.0 / WIDTH) + 1e-05)
    turned = jnp.transpose(trans[...])
    scale = turned[:, 64:65]
    m_high = turned.astype(BF16)
    m_low = (turned - m_high.astype(F32)).astype(BF16)
    for i in range(1, NZ):
        csum_copy(i).wait_recv()
    sums = csum[...].reshape(128, COLS)
    c_high = sums.astype(BF16)
    c_low = (sums - c_high.astype(F32)).astype(BF16)
    part[7] = part[7] + (
        jnp.dot(m_high, c_high, preferred_element_type=F32)
        + jnp.dot(m_low, c_high, preferred_element_type=F32)
        + jnp.dot(m_high, c_low, preferred_element_type=F32)
    )

    for q in range(4):
        rows = pl.ds(q * 64, 64)
        ring_copy(5, q).wait_recv()
        ring_copy(6, q).wait_recv()
        total = part[7, rows, :] + recv3[5, rows, :].astype(F32) + recv3[6, rows, :].astype(F32)
        proj[rows, :] = (total * scale[q * 64 : q * 64 + 64, :]).astype(BF16)

    allowed = mask[...] > 0.5
    for head in range(HEADS):
        base = head * 3 * HD
        query = proj[:, base : base + HD]
        keys = proj[:, base + HD : base + 2 * HD]
        values = proj[:, base + 2 * HD : base + 3 * HD]
        scores = lax.dot_general(query, keys, (((1,), (1,)), ((), ())), preferred_element_type=F32)
        scores = jnp.where(allowed, scores * (1.0 / math.sqrt(HD)), -1e30)
        weights = jnp.exp(scores - jnp.max(scores, axis=1, keepdims=True))
        soft = (weights / jnp.sum(weights, axis=1, keepdims=True)).astype(BF16)
        att[:, head * HD : (head + 1) * HD] = jnp.dot(soft, values, preferred_element_type=F32).astype(BF16)

    spread(att, abuf, s4s, s4r)
    load_o.wait()

    def sum_copy(k, part_of=0):
        if k == 0:
            rows = pl.ds(part_of * 128, 128)
            return copy(send6.at[0, rows], recv6.at[0, rows], s6s.at[0, part_of], s6r.at[0, part_of], along_z(-2 if part_of else 2))
        by = {1: 1, 2: -1, 3: 2, 4: -2, 5: 1, 6: -1}[k]
        return copy(send6.at[k], recv6.at[k], s6s.at[k, 0], s6r.at[k, 0], along_z(by))

    for grp in range(5):
        gather_first(abuf, sems5, s4r, grp)
    gather_second(abuf, sems5, 0)
    gather_second(abuf, sems5, 1)
    gather_last(abuf, sems5, 0)
    product(abuf, 0, wo, part6, 1)
    send6[0] = part6[0].astype(BF16)
    sum_copy(0, 0).start()
    sum_copy(0, 1).start()
    gather_second(abuf, sems5, 2)
    gather_last(abuf, sems5, 1)
    for k in (1, 2):
        product(abuf, k, wo, part6, 1)
        send6[k] = part6[k].astype(BF16)
        sum_copy(k).start()
    gather_second(abuf, sems5, 3)
    gather_last(abuf, sems5, 2)
    for k in (3, 4):
        product(abuf, k, wo, part6, 1)
    gather_second(abuf, sems5, 4)
    gather_last(abuf, sems5, 3)
    for k in (5, 6):
        product(abuf, k, wo, part6, 1)
        send6[k] = part6[k].astype(BF16)
        sum_copy(k).start()
    for k in (3, 4):
        sum_copy(0, k - 3).wait_recv()
        sum_copy(k - 2).wait_recv()
        total = part6[k] + recv6[k - 2].astype(F32)
        send6[k] = total.astype(BF16)
        rows = pl.ds((k - 3) * 128, 128)
        both = part6[k, rows, :] + recv6[k - 2, rows, :].astype(F32) + recv6[0, rows, :].astype(F32)
        send6[k, rows, :] = both.astype(BF16)
        sum_copy(k).start()
    gather_last(abuf, sems5, 4)
    product(abuf, 7, wo, part6, 1)
    total = part6[7] + xin[...].astype(F32)
    for k in (5, 6, 3, 4):
        sum_copy(k).wait_recv()
        total = total + recv6[k].astype(F32)
    result = total.astype(BF16)
    res[...] = result

    @pl.when(s == 0)
    def _():
        hand.start()

    out_ref[0, 0] = result

    spread_drain(xc, xbuf, s1s, s1r)
    spread_drain(att, abuf, s4s, s4r)
    gather_drain(xbuf, sems2)
    gather_drain(abuf, sems5)

    def stat_drain(i, c):
        stat_copy(i).wait_send()
        return c

    lax.fori_loop(1, 16, stat_drain, 0)

    def csum_drain(i, c):
        csum_copy(i).wait_send()
        return c

    lax.fori_loop(1, NZ, csum_drain, 0)
    for k in range(7):
        for q in range(4):
            ring_copy(k, q).wait_send()
    sum_copy(0, 0).wait_send()
    sum_copy(0, 1).wait_send()
    for k in range(1, 7):
        sum_copy(k).wait_send()

    @pl.when(s == 0)
    def _():
        hand.wait_send()


def local(hidden_in, doc_lengths, w_qkv, w_out):
    vmem, dma = pltpu.VMEM, pltpu.SemaphoreType.DMA
    return pl.pallas_call(
        kernel,
        out_shape=jax.ShapeDtypeStruct((1, 1, LEN, FEAT), BF16),
        in_specs=[
            pl.BlockSpec(memory_space=pltpu.SMEM),
            pl.BlockSpec(memory_space=pl.ANY),
            pl.BlockSpec(memory_space=pl.ANY),
            pl.BlockSpec(memory_space=pl.ANY),
        ],
        out_specs=pl.BlockSpec(memory_space=pltpu.VMEM),
        scratch_shapes=[
            vmem((LEN, FEAT), BF16),
            vmem((LEN, FEAT), BF16),
            vmem((ROWS, COLS), BF16),
            vmem((ROWS, FEAT), BF16),
            vmem((16, 8, LEN), F32),
            vmem((16, 8, COLS), F32),
            vmem((128, LEN), F32),
            vmem((LEN, LEN), F32),
            vmem((LEN, COLS), BF16),
            vmem((LEN, FEAT), BF16),
            vmem((LEN, FEAT), BF16),
            vmem((8, 4, 64, ROWS), BF16),
            vmem((8, 4, 64, ROWS), BF16),
            vmem((8, LEN, COLS), F32),
            vmem((7, LEN, COLS), BF16),
            vmem((7, LEN, COLS), BF16),
            vmem((8, LEN, FEAT), F32),
            vmem((7, LEN, FEAT), BF16),
            vmem((7, LEN, FEAT), BF16),
            dma((3,)), dma((2,)),
            dma((16,)), dma((8, 2)), dma((16,)), dma((8, 2)),
            dma((5, 2, 3)), dma((5, 2, 3)), dma((5, 2, 3)), dma((5, 2, 3)),
            dma((5, 2, 3)), dma((5, 2, 3)), dma((5, 2, 3)), dma((5, 2, 3)),
            dma((15,)), dma((15,)), dma((7,)), dma((7,)),
            dma((7, 4)), dma((7, 4)), dma((7, 2)), dma((7, 2)),
        ],
        compiler_params=pltpu.CompilerParams(
            collective_id=0, has_side_effects=True, vmem_limit_bytes=56 * 1024 * 1024
        ),
        cost_estimate=pl.CostEstimate(
            flops=2 * 2048 * ROWS * (COLS + FEAT), bytes_accessed=3 * 1024 * 1024, transcendentals=3 * LEN * LEN
        ),
    )(doc_lengths, hidden_in, w_qkv, w_out)


def solution(mesh):
    return jax.shard_map(
        local,
        mesh=mesh,
        in_specs=(
            P("dp", None, "tensor"),
            P("dp", None),
            P("section", "dp", "tensor"),
            P("section", "dp", "tensor"),
        ),
        out_specs=P("section", "dp", None, "tensor"),
        check_vma=False,
    )
```

```python
import functools
import math

import jax
import jax.numpy as jnp
from jax import lax
from jax.experimental import pallas as pl
from jax.experimental.pallas import tpu as pltpu
from jax.sharding import PartitionSpec as P

MESH = pl.DeviceIdType.MESH
HD = 128
HEADS = 3
LEN = 256
FEAT = 384
ROWS = 768
COLS = 1152
WIDTH = 6144
NZ = 8
GROUPS = ((0, 1), (1, 2), (3, 2), (5, 2), (7, 1))
F32 = jnp.float32
BF16 = jnp.bfloat16


def kernel(
    doc_ref, hid_ref, wq_hbm, wo_hbm, out_ref,
    xin, xc, xc2, wq, wo, stat, stat2, csum, trans, mask, proj, res,
    xbuf, abuf, part, send3, recv3,
    load_sem, hand_sem, go_sem,
    s1s, s1r, a2s, a2r, b2s, b2r, d2s, d2r, a5s, a5r, b5s, b5r,
    t1s, sts, str_, st2s, css, csr, s3s, s3r, wos, wor,
):
    s = lax.axis_index("section")
    t = lax.axis_index("tensor")
    z = lax.axis_index("dp")
    y, x = t // 4, t % 4
    plane = t // 2
    half = t % 2
    at_home = plane == z
    rel = (z - plane + NZ) % NZ
    slot = jnp.where(rel < 4, 7 - 2 * rel, 2 * rel - 8)
    far = (rel >= 3) & (rel <= 5)
    first = s == 0

    def along_z(by):
        return (s, t, (z + by + NZ) % NZ)

    def in_plane(dy, dx):
        return (s, ((y + dy) % 4) * 4 + (x + dx) % 4, z)

    def copy(src, dst, send_sem, recv_sem, device):
        return pltpu.make_async_remote_copy(
            src_ref=src, dst_ref=dst, send_sem=send_sem, recv_sem=recv_sem,
            device_id=device, device_id_type=MESH,
        )

    load_q = pltpu.make_async_copy(wq_hbm.at[0], wq, load_sem.at[0])
    load_o = pltpu.make_async_copy(wo_hbm.at[0], wo.at[z], load_sem.at[1])
    load_x = pltpu.make_async_copy(hid_ref.at[0], xin, load_sem.at[2])

    @pl.when(s == 0)
    def _():
        load_x.start()

    load_q.start()
    load_o.start()

    barrier = pltpu.get_barrier_semaphore()

    def greet(device):
        pl.semaphore_signal(barrier, inc=1, device_id=device, device_id_type=MESH)

    def greet_source(i, c):
        source_t, source_z = 2 * z + i % 2, i // 2

        @pl.when(jnp.logical_not(first & (source_t == t) & (source_z == z)))
        def _():
            greet((0, source_t, source_z))

        return c

    lax.fori_loop(0, 16, greet_source, 0)

    def greet_plane(i, c):
        greet(in_plane(i // 4, i % 4))
        return c

    lax.fori_loop(1, 16, greet_plane, 0)

    def greet_line(i, c):
        greet(along_z(i))
        return c

    lax.fori_loop(1, NZ, greet_line, 0)

    @pl.when(s == 1)
    def _():
        def greet_before(i, c):
            greet((0, i, z))
            return c

        lax.fori_loop(0, 16, greet_before, 0)

    load_q.wait()
    row16 = lax.broadcasted_iota(jnp.int32, (16, ROWS), 0)
    col16 = lax.broadcasted_iota(jnp.int32, (16, ROWS), 1)
    pick = jnp.where(row16 == col16 // FEAT, 1.0, 0.0).astype(BF16)
    csum[z] = jnp.dot(pick, wq[...], preferred_element_type=F32)[0:8, :]
    csum[NZ : 2 * NZ] = jnp.zeros((NZ, 8, COLS), F32)

    def csum_copy(i):
        return copy(csum.at[z], csum.at[z], css.at[i - 1], csr.at[i - 1], along_z(i))

    def csum_send(i, c):
        csum_copy(i).start()
        return c

    def centre(value):
        own_mean = jnp.mean(value, axis=1, keepdims=True)
        off = value - own_mean
        own_sq = jnp.sum(off * off, axis=1, keepdims=True)
        lane = lax.broadcasted_iota(jnp.int32, (LEN, 128), 1)
        columns = jnp.where(lane == 0, own_mean, jnp.where(lane == 1, own_sq, 0.0))
        return off.astype(BF16), jnp.transpose(columns)[0:8, :]

    def stat_copy(i):
        return copy(stat.at[t], stat.at[t], sts.at[i - 1], str_.at[i], in_plane(i // 4, i % 4))

    def stat_send(i, c):
        stat_copy(i).start()
        return c

    def stat_on_copy(i):
        _, there, same_z = in_plane(i // 4, i % 4)
        return copy(stat2, stat.at[t], st2s.at[i], str_.at[i], (1, there, same_z))

    def stat_on_send(i, c):
        stat_on_copy(i).start()
        return c

    def hand():
        return copy(res, xin, hand_sem.at[0], hand_sem.at[1], (1, t, z))

    @pl.when(first)
    def _():
        load_x.wait()
        low, rows = centre(xin[...].astype(F32))
        xc[...] = low
        stat[t] = rows

    pl.semaphore_wait(barrier, jnp.where(first, 16 + 16 + 16 - at_home.astype(jnp.int32), 0) + 15 + 7)

    def spread_copy(src, buf, ssem, rsem, to, g):
        rows = pl.ds(pl.multiple_of(g * 16, 16), 16)
        there = pl.ds(pl.multiple_of((g % 4) * 16, 16), 16)
        cols = pl.ds(pl.multiple_of(half * FEAT, 128), FEAT)
        from_ref, to_ref = src.at[rows, :], buf.at[slot, g // 4, there, cols]

        def remote():
            return copy(from_ref, to_ref, ssem.at[g], rsem.at[slot, half], (to, g, plane))

        def local():
            return pltpu.make_async_copy(from_ref, to_ref, rsem.at[slot, half])

        return remote, local

    def spread(src, buf, ssem, rsem, to, other_core=False):
        def body(g, c):
            remote, local = spread_copy(src, buf, ssem, rsem, to, g)
            if other_core:
                remote().start()
                return c
            own = at_home & (g == t)

            @pl.when(own)
            def _():
                local().start()

            @pl.when(jnp.logical_not(own))
            def _():
                remote().start()

            return c

        lax.fori_loop(0, 16, body, 0)

    def spread_drain(src, buf, ssem, rsem, to, other_core=False):
        def body(g, c):
            remote, _ = spread_copy(src, buf, ssem, rsem, to, g)
            if other_core:
                remote().wait_send()
                return c

            @pl.when(jnp.logical_not(at_home & (g == t)))
            def _():
                remote().wait_send()

            return c

        lax.fori_loop(0, 16, body, 0)

    def spread_wait(buf, rsem, k, h):
        there = buf.at[k, y, pl.ds(pl.multiple_of(x * 16, 16), 16), pl.ds(h * FEAT, FEAT)]
        pltpu.make_async_copy(there, there, rsem.at[k, h]).wait()

    def gather_copy(buf, sems, step, grp, h, j):
        k0, n = GROUPS[grp]
        own = pl.ds(pl.multiple_of(x * 16, 16), 16)
        cols = pl.ds(h * FEAT, FEAT)
        if step == 0:
            ref = buf.at[pl.ds(k0, n), y, own, cols]
        elif h == 0:
            ref = buf.at[pl.ds(k0, n), y, :, cols]
        else:
            ref = buf.at[pl.ds(k0, n), :, own, cols]
        device = in_plane(0, j) if (step == h) else in_plane(j, 0)
        return copy(ref, ref, sems[2 * step].at[grp, h, j - 1], sems[2 * step + 1].at[grp, h, j - 1], device)

    def direct_copy(buf, sems, i):
        ref = buf.at[0, y, pl.ds(pl.multiple_of(x * 16, 16), 16), :]
        return copy(ref, ref, sems[4].at[i - 1], sems[5].at[i - 1], in_plane(i // 4, i % 4))

    def gather_direct(buf, sems, rsem):
        spread_wait(buf, rsem, 0, 0)
        spread_wait(buf, rsem, 0, 1)

        def body(i, c):
            direct_copy(buf, sems, 16 - i).start()
            return c

        lax.fori_loop(1, 16, body, 0)

    def direct_wait(buf, sems):
        def body(i, c):
            direct_copy(buf, sems, i).wait_recv()
            return c

        lax.fori_loop(1, 16, body, 0)

    def gather_first(buf, sems, rsem, grp):
        k0, n = GROUPS[grp]
        for h in range(2):
            for k in range(k0, k0 + n):
                spread_wait(buf, rsem, k, h)
            for j in (2, 1, 3):
                gather_copy(buf, sems, 0, grp, h, j).start()

    def gather_second(buf, sems, grp):
        for h in range(2):
            for j in (1, 2, 3):
                gather_copy(buf, sems, 0, grp, h, j).wait_recv()
            for j in (2, 1, 3):
                gather_copy(buf, sems, 1, grp, h, j).start()

    def gather_last(buf, sems, grp):
        for h in range(2):
            for j in (1, 2, 3):
                gather_copy(buf, sems, 1, grp, h, j).wait_recv()

    def gather_drain(buf, sems):
        def body(i, c):
            direct_copy(buf, sems, i).wait_send()
            return c

        lax.fori_loop(1, 16, body, 0)
        for grp in range(1, len(GROUPS)):
            for step in range(2):
                for h in range(2):
                    for j in (1, 2, 3):
                        gather_copy(buf, sems, step, grp, h, j).wait_send()

    @pl.when(first & far)
    def _():
        spread(xc, xbuf, s1s, s1r, 0)

    @pl.when(first)
    def _():
        lax.fori_loop(1, 16, stat_send, 0)

    lax.fori_loop(1, NZ, csum_send, 0)

    @pl.when(first & jnp.logical_not(far))
    def _():
        spread(xc, xbuf, s1s, s1r, 0)

    sems2 = (a2s, a2r, b2s, b2r, d2s, d2r)

    def weight_copy(step, way):
        chunk = (z + (step if way else -step) + NZ) % NZ
        if step == 3:
            rows = pl.ds(FEAT if way else 0, FEAT)
            ref = wo.at[chunk, rows]
        else:
            ref = wo.at[chunk]
        return copy(ref, ref, wos.at[way, step], wor.at[way, step], along_z(-1 if way else 1))

    def weight_step(step):
        for way in range(2):
            if step:
                weight_copy(step - 1, way).wait_recv()
            if step < 4:
                weight_copy(step, way).start()

    @pl.when(s == 1)
    def _():
        pl.semaphore_wait(go_sem, 1)

    load_o.wait()
    weight_step(0)

    def product(buf, k, w, into, tiles):
        rows = buf[k].reshape(LEN, ROWS)

        def body(n, c):
            cols = pl.ds(pl.multiple_of(n * FEAT, 128), FEAT)
            into[k, :, cols] = jnp.dot(rows, w[:, cols], preferred_element_type=F32)
            return c

        lax.fori_loop(0, tiles, body, 0)

    def ring_copy(k, q):
        rows = pl.ds(q * 64, 64)
        up = q < 2 if k == 0 else k % 2 == 1
        return copy(send3.at[k, rows], recv3.at[k, rows], s3s.at[k, q], s3r.at[k, q], along_z(1 if up else -1))

    def ring_step(k, q, before):
        rows = pl.ds(q * 64, 64)
        value = part[k, rows, :]
        if before is not None:
            ring_copy(before, q).wait_recv()
            value = value + recv3[before, rows, :].astype(F32)
        send3[k, rows, :] = value.astype(BF16)
        ring_copy(k, q).start()

    gather_direct(xbuf, sems2, s1r)
    for grp in range(1, 5):
        gather_first(xbuf, sems2, s1r, grp)

    weight_step(1)

    row_pos = lax.broadcasted_iota(jnp.int32, (LEN, LEN), 0)
    col_pos = lax.broadcasted_iota(jnp.int32, (LEN, LEN), 1)
    row_doc = jnp.zeros((LEN, LEN), jnp.int32)
    col_doc = jnp.zeros((LEN, LEN), jnp.int32)
    end = jnp.int32(0)
    for i in range(4):
        end = end + doc_ref[0, i]
        row_doc = row_doc + (row_pos >= end).astype(jnp.int32)
        col_doc = col_doc + (col_pos >= end).astype(jnp.int32)
    mask[...] = jnp.where((col_pos <= row_pos) & (row_doc == col_doc), 1.0, 0.0)

    gather_second(xbuf, sems2, 1)
    direct_wait(xbuf, sems2)
    product(xbuf, 0, wq, part, 3)
    for q in (0, 2, 1, 3):
        ring_step(0, q, None)
    gather_second(xbuf, sems2, 2)
    gather_last(xbuf, sems2, 1)
    product(xbuf, 1, wq, part, 3)
    ring_step(1, 2, None)
    ring_step(1, 3, None)
    product(xbuf, 2, wq, part, 3)
    ring_step(2, 0, None)
    ring_step(2, 1, None)
    gather_second(xbuf, sems2, 3)
    gather_last(xbuf, sems2, 2)
    product(xbuf, 3, wq, part, 3)
    product(xbuf, 4, wq, part, 3)
    ring_step(1, 0, 0)
    ring_step(2, 2, 0)
    ring_step(1, 1, 0)
    ring_step(2, 3, 0)
    gather_second(xbuf, sems2, 4)
    gather_last(xbuf, sems2, 3)
    product(xbuf, 5, wq, part, 3)
    product(xbuf, 6, wq, part, 3)
    up_order, down_order = (2, 3, 0, 1), (0, 1, 2, 3)
    for i in range(4):
        ring_step(3, up_order[i], 1)
        ring_step(4, down_order[i], 2)
    gather_last(xbuf, sems2, 4)
    product(xbuf, 7, wq, part, 3)
    for i in range(4):
        ring_step(5, up_order[i], 3)
        ring_step(6, down_order[i], 4)

    @pl.when(first)
    def _():
        pl.semaphore_signal(go_sem, inc=1, device_id=(1, t, z), device_id_type=MESH)

    for i in range(1, 16):
        stat_copy(i).wait_recv()

    @pl.when(s == 1)
    def _():
        stat_on_copy(0).wait_recv()

    means = [stat[i, 0:1, :] for i in range(16)]
    mean = functools.reduce(lambda a, b: a + b, means) * (1.0 / 16)
    square = functools.reduce(lambda a, b: a + b, [stat[i, 1:2, :] for i in range(16)])
    trans[...] = jnp.zeros((128, LEN), F32)
    for i in range(16):
        off = means[i] - mean
        square = square + FEAT * (off * off)
        trans[pl.ds((i // 2) * 8 + i % 2, 1), :] = off
    trans[pl.ds(64, 1), :] = lax.rsqrt(square * (1.0 / WIDTH) + 1e-05)
    turned = jnp.transpose(trans[...])
    scale = turned[:, 64:65]
    m_high = turned.astype(BF16)
    m_low = (turned - m_high.astype(F32)).astype(BF16)
    for i in range(1, NZ):
        csum_copy(i).wait_recv()
    sums = csum[...].reshape(128, COLS)
    c_high = sums.astype(BF16)
    c_low = (sums - c_high.astype(F32)).astype(BF16)
    part[7] = part[7] + (
        jnp.dot(m_high, c_high, preferred_element_type=F32)
        + jnp.dot(m_low, c_high, preferred_element_type=F32)
        + jnp.dot(m_high, c_low, preferred_element_type=F32)
    )

    for q in range(4):
        rows = pl.ds(q * 64, 64)
        ring_copy(5, q).wait_recv()
        ring_copy(6, q).wait_recv()
        total = part[7, rows, :] + recv3[5, rows, :].astype(F32) + recv3[6, rows, :].astype(F32)
        proj[rows, :] = (total * scale[q * 64 : q * 64 + 64, :]).astype(BF16)

    weight_step(2)

    def head_copy(step, head, h, j):
        rows = pl.ds(h * 128, 128)
        own = pl.ds(pl.multiple_of((x % 2) * HD, 128), HD)
        if step == 0:
            ref = abuf.at[head, y, x // 2, rows, own]
        elif h == 0:
            ref = abuf.at[head, y, :, rows]
        else:
            ref = abuf.at[head, :, x // 2, rows, own]
        device = in_plane(0, j) if (step == h) else in_plane(j, 0)
        send, recv = (b5s, b5r) if step else (a5s, a5r)
        return copy(ref, ref, send.at[head, h, j - 1], recv.at[head, h, j - 1], device)

    allowed = mask[...] > 0.5
    for head in range(HEADS):
        base = head * 3 * HD
        query = proj[:, base : base + HD]
        keys = proj[:, base + HD : base + 2 * HD]
        values = proj[:, base + 2 * HD : base + 3 * HD]
        scores = lax.dot_general(query, keys, (((1,), (1,)), ((), ())), preferred_element_type=F32)
        scores = jnp.where(allowed, scores * (1.0 / math.sqrt(HD)), -1e30)
        weights = jnp.exp(scores - jnp.max(scores, axis=1, keepdims=True))
        soft = (weights / jnp.sum(weights, axis=1, keepdims=True)).astype(BF16)
        ahead = jnp.dot(soft, values, preferred_element_type=F32).astype(BF16)
        abuf[head, y, x // 2, :, pl.ds(pl.multiple_of((x % 2) * HD, 128), HD)] = ahead
        for h in range(2):
            for j in (2, 1, 3):
                head_copy(0, head, h, j).start()

    @pl.when(first)
    def _():
        spread_drain(xc, xbuf, s1s, s1r, 0)

        def stat_drain(i, c):
            stat_copy(i).wait_send()
            return c

        lax.fori_loop(1, 16, stat_drain, 0)

    weight_step(3)
    for head in range(HEADS):
        for h in range(2):
            for j in (1, 2, 3):
                head_copy(0, head, h, j).wait_recv()
            for j in (2, 1, 3):
                head_copy(1, head, h, j).start()

    gather_drain(xbuf, sems2)

    def csum_drain(i, c):
        csum_copy(i).wait_send()
        return c

    lax.fori_loop(1, NZ, csum_drain, 0)
    for k in range(7):
        for q in range(4):
            ring_copy(k, q).wait_send()
    weight_step(4)
    for step in range(4):
        for way in range(2):
            weight_copy(step, way).wait_send()
    for head in range(HEADS):
        for h in range(2):
            for j in (1, 2, 3):
                head_copy(0, head, h, j).wait_send()

    @pl.when(s == 1)
    def _():
        hand().wait_recv()

    total = xin[...].astype(F32)
    for head in range(HEADS):
        for h in range(2):
            for j in (1, 2, 3):
                head_copy(1, head, h, j).wait_recv()
        for d in range(NZ):
            rows = jnp.concatenate([wo[d, head * HD : head * HD + HD], wo[d, FEAT + head * HD : FEAT + head * HD + HD]], axis=0)
            total = total + jnp.dot(abuf[head, d // 2, d % 2], rows, preferred_element_type=F32)
    result = total.astype(BF16)
    res[...] = result

    @pl.when(first)
    def _():
        low, rows = centre(res[...].astype(F32))
        xc2[...] = low
        stat2[...] = rows

        @pl.when(far)
        def _():
            spread(xc2, xbuf, t1s, s1r, 1, True)

        lax.fori_loop(0, 16, stat_on_send, 0)
        hand().start()

        @pl.when(jnp.logical_not(far))
        def _():
            spread(xc2, xbuf, t1s, s1r, 1, True)

    out_ref[0, 0] = res[...]
    for head in range(HEADS):
        for h in range(2):
            for j in (1, 2, 3):
                head_copy(1, head, h, j).wait_send()

    @pl.when(first)
    def _():
        spread_drain(xc2, xbuf, t1s, s1r, 1, True)

        def stat_on_drain(i, c):
            stat_on_copy(i).wait_send()
            return c

        lax.fori_loop(0, 16, stat_on_drain, 0)
        hand().wait_send()


def local(hidden_in, doc_lengths, w_qkv, w_out):
    vmem, dma = pltpu.VMEM, pltpu.SemaphoreType.DMA
    return pl.pallas_call(
        kernel,
        out_shape=jax.ShapeDtypeStruct((1, 1, LEN, FEAT), BF16),
        in_specs=[
            pl.BlockSpec(memory_space=pltpu.SMEM),
            pl.BlockSpec(memory_space=pl.ANY),
            pl.BlockSpec(memory_space=pl.ANY),
            pl.BlockSpec(memory_space=pl.ANY),
        ],
        out_specs=pl.BlockSpec(memory_space=pltpu.VMEM),
        scratch_shapes=[
            vmem((LEN, FEAT), BF16),
            vmem((LEN, FEAT), BF16),
            vmem((LEN, FEAT), BF16),
            vmem((ROWS, COLS), BF16),
            vmem((NZ, ROWS, FEAT), BF16),
            vmem((16, 8, LEN), F32),
            vmem((8, LEN), F32),
            vmem((16, 8, COLS), F32),
            vmem((128, LEN), F32),
            vmem((LEN, LEN), F32),
            vmem((LEN, COLS), BF16),
            vmem((LEN, FEAT), BF16),
            vmem((8, 4, 64, ROWS), BF16),
            vmem((HEADS, 4, 2, LEN, 2 * HD), BF16),
            vmem((8, LEN, COLS), F32),
            vmem((7, LEN, COLS), BF16),
            vmem((7, LEN, COLS), BF16),
            dma((3,)), dma((2,)), pltpu.SemaphoreType.REGULAR,
            dma((16,)), dma((8, 2)),
            dma((5, 2, 3)), dma((5, 2, 3)), dma((5, 2, 3)), dma((5, 2, 3)), dma((15,)), dma((15,)),
            dma((3, 2, 3)), dma((3, 2, 3)), dma((3, 2, 3)), dma((3, 2, 3)),
            dma((16,)), dma((15,)), dma((16,)), dma((16,)), dma((7,)), dma((7,)),
            dma((7, 4)), dma((7, 4)), dma((2, 4)), dma((2, 4)),
        ],
        compiler_params=pltpu.CompilerParams(
            collective_id=0, has_side_effects=True, vmem_limit_bytes=56 * 1024 * 1024
        ),
        cost_estimate=pl.CostEstimate(
            flops=2 * 2048 * ROWS * (COLS + FEAT), bytes_accessed=3 * 1024 * 1024, transcendentals=3 * LEN * LEN
        ),
    )(doc_lengths, hidden_in, w_qkv, w_out)


def solution(mesh):
    return jax.shard_map(
        local,
        mesh=mesh,
        in_specs=(
            P("dp", None, "tensor"),
            P("dp", None),
            P("section", "dp", "tensor"),
            P("section", "dp", "tensor"),
        ),
        out_specs=P("section", "dp", None, "tensor"),
        check_vma=False,
    )
```

```python
import functools
import math

import jax
import jax.numpy as jnp
from jax import lax
from jax.experimental import pallas as pl
from jax.experimental.pallas import tpu as pltpu
from jax.sharding import PartitionSpec as P

MESH = pl.DeviceIdType.MESH
HD = 128
HEADS = 3
LEN = 256
FEAT = 384
ROWS = 768
COLS = 1152
WIDTH = 6144
NZ = 8
GROUPS = ((0, 1), (1, 2), (3, 2), (5, 2), (7, 1))
F32 = jnp.float32
BF16 = jnp.bfloat16


def kernel(
    doc_ref, hid_ref, wq_hbm, wo_hbm, out_ref,
    xin, wq, wo, turn, norm, mask, proj, res,
    xbuf, abuf, part, send3, recv3,
    load_sem, hand_sem, go_sem,
    t1s, t1r, t2s, s1s, s1r, a2s, a2r, b2s, b2r, a5s, a5r, b5s, b5r,
    s3s, s3r, wos, wor,
):
    s = lax.axis_index("section")
    t = lax.axis_index("tensor")
    z = lax.axis_index("dp")
    y, x = t // 4, t % 4
    first = s == 0

    def along_z(by):
        return (s, t, (z + by + NZ) % NZ)

    def in_plane(dy, dx):
        return (s, ((y + dy) % 4) * 4 + (x + dx) % 4, z)

    def copy(src, dst, send_sem, recv_sem, device):
        return pltpu.make_async_remote_copy(
            src_ref=src, dst_ref=dst, send_sem=send_sem, recv_sem=recv_sem,
            device_id=device, device_id_type=MESH,
        )

    load_q = pltpu.make_async_copy(wq_hbm.at[0], wq, load_sem.at[0])
    load_o = pltpu.make_async_copy(wo_hbm.at[0], wo.at[z], load_sem.at[1])
    load_x = pltpu.make_async_copy(hid_ref.at[0], xin, load_sem.at[2])

    @pl.when(s == 0)
    def _():
        load_x.start()

    load_q.start()
    load_o.start()

    barrier = pltpu.get_barrier_semaphore()

    def greet(device):
        pl.semaphore_signal(barrier, inc=1, device_id=device, device_id_type=MESH)

    def greet_plane(i, c):
        greet(in_plane(i // 4, i % 4))
        return c

    lax.fori_loop(1, 16, greet_plane, 0)

    def greet_line(i, c):
        greet(along_z(i))
        return c

    lax.fori_loop(1, NZ, greet_line, 0)

    @pl.when(s == 1)
    def _():
        def greet_before(i, c):
            greet((0, i, z))
            return c

        lax.fori_loop(0, 16, greet_before, 0)

    def hand():
        return copy(res, xin, hand_sem.at[0], hand_sem.at[1], (1, t, z))

    @pl.when(first)
    def _():
        load_x.wait()

    pl.semaphore_wait(barrier, jnp.where(first, 16, 0) + 15 + 7)

    def turn_copy(src, i, to):
        _, g, _ = in_plane(i // 4, i % 4)
        rows = pl.ds(pl.multiple_of(g * 16, 16), 16)
        cols = pl.ds(pl.multiple_of((t % 2) * FEAT, 128), FEAT)
        sems = t1s if to == 0 else t2s
        return copy(src.at[rows, :], turn.at[t // 2, :, cols], sems.at[i], t1r.at[i], (to, g, z))

    def turn_send(src, to):
        def body(i, c):
            turn_copy(src, i, to).start()
            return c

        lax.fori_loop(1 - to, 16, body, 0)

    def turn_drain(src, to):
        def body(i, c):
            turn_copy(src, i, to).wait_send()
            return c

        lax.fori_loop(1 - to, 16, body, 0)

    own_rows = pl.ds(pl.multiple_of(x * 16, 16), 16)

    def line_copy(k):
        by = (4, -3, 3, -2, 2, -1, 1)[k]
        device = along_z(by)
        return copy(norm.at[device[2]], xbuf.at[k, y, own_rows, :], s1s.at[k], s1r.at[k], device)

    def line_wait(k):
        there = xbuf.at[k, y, own_rows, :]
        pltpu.make_async_copy(there, there, s1r.at[k]).wait()

    def gather_copy(buf, sems, step, grp, h, j):
        k0, n = GROUPS[grp]
        own = pl.ds(pl.multiple_of(x * 16, 16), 16)
        cols = pl.ds(h * FEAT, FEAT)
        if step == 0:
            ref = buf.at[pl.ds(k0, n), y, own, cols]
        elif h == 0:
            ref = buf.at[pl.ds(k0, n), y, :, cols]
        else:
            ref = buf.at[pl.ds(k0, n), :, own, cols]
        device = in_plane(0, j) if (step == h) else in_plane(j, 0)
        return copy(ref, ref, sems[2 * step].at[grp, h, j - 1], sems[2 * step + 1].at[grp, h, j - 1], device)

    def gather_first(buf, sems, grp):
        k0, n = GROUPS[grp]
        for k in range(k0, min(k0 + n, 7)):
            line_wait(k)
        for h in range(2):
            for j in (2, 1, 3):
                gather_copy(buf, sems, 0, grp, h, j).start()

    def gather_second(buf, sems, grp):
        for h in range(2):
            for j in (1, 2, 3):
                gather_copy(buf, sems, 0, grp, h, j).wait_recv()
            for j in (2, 1, 3):
                gather_copy(buf, sems, 1, grp, h, j).start()

    def gather_last(buf, sems, grp):
        for h in range(2):
            for j in (1, 2, 3):
                gather_copy(buf, sems, 1, grp, h, j).wait_recv()

    def gather_drain(buf, sems):
        for grp in range(len(GROUPS)):
            for step in range(2):
                for h in range(2):
                    for j in (1, 2, 3):
                        gather_copy(buf, sems, step, grp, h, j).wait_send()

    @pl.when(first)
    def _():
        rows = pl.ds(pl.multiple_of(t * 16, 16), 16)
        turn[t // 2, :, pl.ds(pl.multiple_of((t % 2) * FEAT, 128), FEAT)] = xin[rows, :]
        turn_send(xin, 0)

    sems2 = (a2s, a2r, b2s, b2r)

    def weight_copy(step, way, part_of):
        chunk = (z + (step if way else -step) + NZ) % NZ
        near = way if part_of == 0 else 1 - way
        ref = wo.at[chunk, pl.ds(near * FEAT, FEAT)]
        return copy(ref, ref, wos.at[way, step, part_of], wor.at[way, step, part_of], along_z(-1 if way else 1))

    def weight_step(step):
        for part_of in range(2):
            for way in range(2):
                if step and (step, part_of) != (3, 1):
                    before = 2 if (step, part_of) == (4, 1) else step - 1
                    weight_copy(before, way, part_of).wait_recv()
                if step < 3 or (step == 3 and part_of == 0):
                    weight_copy(step, way, part_of).start()

    def weight_drain():
        for step in range(4):
            for way in range(2):
                weight_copy(step, way, 0).wait_send()
                if step < 3:
                    weight_copy(step, way, 1).wait_send()

    def product(buf, k, w, into, tiles):
        rows = buf[k].reshape(LEN, ROWS)

        def body(n, c):
            cols = pl.ds(pl.multiple_of(n * FEAT, 128), FEAT)
            into[k, :, cols] = jnp.dot(rows, w[:, cols], preferred_element_type=F32)
            return c

        lax.fori_loop(0, tiles, body, 0)

    def ring_copy(k, q):
        rows = pl.ds(q * 64, 64)
        up = q < 2 if k == 0 else k % 2 == 1
        return copy(send3.at[k, rows], recv3.at[k, rows], s3s.at[k, q], s3r.at[k, q], along_z(1 if up else -1))

    def ring_step(k, q, before):
        rows = pl.ds(q * 64, 64)
        value = part[k, rows, :]
        if before is not None:
            ring_copy(before, q).wait_recv()
            value = value + recv3[before, rows, :].astype(F32)
        send3[k, rows, :] = value.astype(BF16)
        ring_copy(k, q).start()

    @pl.when(s == 1)
    def _():
        pl.semaphore_wait(go_sem, 1)

    load_o.wait()
    weight_step(0)

    for i in range(1, 16):
        turn_copy(xin, i, 0).wait_recv()

    @pl.when(s == 1)
    def _():
        turn_copy(xin, 0, 0).wait_recv()

    whole = turn[...].astype(F32)
    mean = jnp.sum(jnp.sum(whole, axis=0), axis=1, keepdims=True) * (1.0 / WIDTH)
    off = whole - mean[None]
    spread = jnp.sum(jnp.sum(off * off, axis=0), axis=1, keepdims=True) * (1.0 / WIDTH)
    norm[...] = (off * lax.rsqrt(spread + 1e-05)[None]).astype(BF16)
    for k in range(7):
        line_copy(k).start()
    xbuf[7, y, own_rows, :] = norm[z]

    for grp in range(0, 5):
        gather_first(xbuf, sems2, grp)

    weight_step(1)

    row_pos = lax.broadcasted_iota(jnp.int32, (LEN, LEN), 0)
    col_pos = lax.broadcasted_iota(jnp.int32, (LEN, LEN), 1)
    row_doc = jnp.zeros((LEN, LEN), jnp.int32)
    col_doc = jnp.zeros((LEN, LEN), jnp.int32)
    end = jnp.int32(0)
    for i in range(4):
        end = end + doc_ref[0, i]
        row_doc = row_doc + (row_pos >= end).astype(jnp.int32)
        col_doc = col_doc + (col_pos >= end).astype(jnp.int32)
    mask[...] = jnp.where((col_pos <= row_pos) & (row_doc == col_doc), 1.0, 0.0)

    gather_second(xbuf, sems2, 0)
    gather_second(xbuf, sems2, 1)
    load_q.wait()
    gather_last(xbuf, sems2, 0)
    product(xbuf, 0, wq, part, 3)
    for q in (0, 2, 1, 3):
        ring_step(0, q, None)
    gather_second(xbuf, sems2, 2)
    gather_last(xbuf, sems2, 1)
    product(xbuf, 1, wq, part, 3)
    ring_step(1, 2, None)
    ring_step(1, 3, None)
    product(xbuf, 2, wq, part, 3)
    ring_step(2, 0, None)
    ring_step(2, 1, None)
    gather_second(xbuf, sems2, 3)
    gather_last(xbuf, sems2, 2)
    product(xbuf, 3, wq, part, 3)
    product(xbuf, 4, wq, part, 3)
    ring_step(1, 0, 0)
    ring_step(2, 2, 0)
    ring_step(1, 1, 0)
    ring_step(2, 3, 0)
    gather_second(xbuf, sems2, 4)
    gather_last(xbuf, sems2, 3)
    product(xbuf, 5, wq, part, 3)
    product(xbuf, 6, wq, part, 3)
    up_order, down_order = (2, 3, 0, 1), (0, 1, 2, 3)
    for i in range(4):
        ring_step(3, up_order[i], 1)
        ring_step(4, down_order[i], 2)
    gather_last(xbuf, sems2, 4)
    product(xbuf, 7, wq, part, 3)
    for i in range(4):
        ring_step(5, up_order[i], 3)
        ring_step(6, down_order[i], 4)

    weight_step(2)
    for q in range(4):
        rows = pl.ds(q * 64, 64)
        ring_copy(5, q).wait_recv()
        ring_copy(6, q).wait_recv()
        total = part[7, rows, :] + recv3[5, rows, :].astype(F32) + recv3[6, rows, :].astype(F32)
        proj[rows, :] = total.astype(BF16)

    def head_copy(step, head, h, j):
        rows = pl.ds(h * 128, 128)
        own = pl.ds(pl.multiple_of((x % 2) * HD, 128), HD)
        if step == 0:
            ref = abuf.at[head, y, x // 2, rows, own]
        elif h == 0:
            ref = abuf.at[head, y, :, rows]
        else:
            ref = abuf.at[head, :, x // 2, rows, own]
        device = in_plane(0, j) if (step == h) else in_plane(j, 0)
        send, recv = (b5s, b5r) if step else (a5s, a5r)
        return copy(ref, ref, send.at[head, h, j - 1], recv.at[head, h, j - 1], device)

    allowed = mask[...] > 0.5
    for head in range(HEADS):
        base = head * 3 * HD
        query = proj[:, base : base + HD]
        keys = proj[:, base + HD : base + 2 * HD]
        values = proj[:, base + 2 * HD : base + 3 * HD]
        scores = lax.dot_general(query, keys, (((1,), (1,)), ((), ())), preferred_element_type=F32)
        scores = jnp.where(allowed, scores * (1.0 / math.sqrt(HD)), -1e30)
        weights = jnp.exp(scores - jnp.max(scores, axis=1, keepdims=True))
        soft = (weights / jnp.sum(weights, axis=1, keepdims=True)).astype(BF16)
        ahead = jnp.dot(soft, values, preferred_element_type=F32).astype(BF16)
        abuf[head, y, x // 2, :, pl.ds(pl.multiple_of((x % 2) * HD, 128), HD)] = ahead
        for h in range(2):
            for j in (2, 1, 3):
                head_copy(0, head, h, j).start()

    @pl.when(first)
    def _():
        turn_drain(xin, 0)

    for k in range(7):
        line_copy(k).wait_send()
    weight_step(3)
    for head in range(HEADS):
        for h in range(2):
            for j in (1, 2, 3):
                head_copy(0, head, h, j).wait_recv()
            for j in (2, 1, 3):
                head_copy(1, head, h, j).start()

    gather_drain(xbuf, sems2)

    for k in range(7):
        for q in range(4):
            ring_copy(k, q).wait_send()
    weight_step(4)

    @pl.when(first)
    def _():
        pl.semaphore_signal(go_sem, inc=1, device_id=(1, t, z), device_id_type=MESH)

    weight_drain()
    for head in range(HEADS):
        for h in range(2):
            for j in (1, 2, 3):
                head_copy(0, head, h, j).wait_send()

    @pl.when(s == 1)
    def _():
        hand().wait_recv()

    total = xin[...].astype(F32)
    for head in range(HEADS):
        for h in range(2):
            for j in (1, 2, 3):
                head_copy(1, head, h, j).wait_recv()
        for d in range(NZ):
            rows = jnp.concatenate([wo[d, head * HD : head * HD + HD], wo[d, FEAT + head * HD : FEAT + head * HD + HD]], axis=0)
            total = total + jnp.dot(abuf[head, d // 2, d % 2], rows, preferred_element_type=F32)
    result = total.astype(BF16)
    res[...] = result

    @pl.when(first)
    def _():
        turn_send(res, 1)
        hand().start()

    out_ref[0, 0] = res[...]
    for head in range(HEADS):
        for h in range(2):
            for j in (1, 2, 3):
                head_copy(1, head, h, j).wait_send()

    @pl.when(first)
    def _():
        turn_drain(res, 1)
        hand().wait_send()


def local(hidden_in, doc_lengths, w_qkv, w_out):
    vmem, dma = pltpu.VMEM, pltpu.SemaphoreType.DMA
    return pl.pallas_call(
        kernel,
        out_shape=jax.ShapeDtypeStruct((1, 1, LEN, FEAT), BF16),
        in_specs=[
            pl.BlockSpec(memory_space=pltpu.SMEM),
            pl.BlockSpec(memory_space=pl.ANY),
            pl.BlockSpec(memory_space=pl.ANY),
            pl.BlockSpec(memory_space=pl.ANY),
        ],
        out_specs=pl.BlockSpec(memory_space=pltpu.VMEM),
        scratch_shapes=[
            vmem((LEN, FEAT), BF16),
            vmem((ROWS, COLS), BF16),
            vmem((NZ, ROWS, FEAT), BF16),
            vmem((NZ, 16, ROWS), BF16),
            vmem((NZ, 16, ROWS), BF16),
            vmem((LEN, LEN), F32),
            vmem((LEN, COLS), BF16),
            vmem((LEN, FEAT), BF16),
            vmem((8, 4, 64, ROWS), BF16),
            vmem((HEADS, 4, 2, LEN, 2 * HD), BF16),
            vmem((8, LEN, COLS), F32),
            vmem((7, LEN, COLS), BF16),
            vmem((7, LEN, COLS), BF16),
            dma((3,)), dma((2,)), pltpu.SemaphoreType.REGULAR,
            dma((16,)), dma((16,)), dma((16,)), dma((7,)), dma((7,)),
            dma((5, 2, 3)), dma((5, 2, 3)), dma((5, 2, 3)), dma((5, 2, 3)),
            dma((3, 2, 3)), dma((3, 2, 3)), dma((3, 2, 3)), dma((3, 2, 3)),
            dma((7, 4)), dma((7, 4)), dma((2, 4, 2)), dma((2, 4, 2)),
        ],
        compiler_params=pltpu.CompilerParams(
            collective_id=0, has_side_effects=True, vmem_limit_bytes=56 * 1024 * 1024
        ),
        cost_estimate=pl.CostEstimate(
            flops=2 * 2048 * ROWS * (COLS + FEAT), bytes_accessed=3 * 1024 * 1024, transcendentals=3 * LEN * LEN
        ),
    )(doc_lengths, hidden_in, w_qkv, w_out)


def solution(mesh):
    return jax.shard_map(
        local,
        mesh=mesh,
        in_specs=(
            P("dp", None, "tensor"),
            P("dp", None),
            P("section", "dp", "tensor"),
            P("section", "dp", "tensor"),
        ),
        out_specs=P("section", "dp", None, "tensor"),
        check_vma=False,
    )
```

```python
import functools
import math

import jax
import jax.numpy as jnp
from jax import lax
from jax.experimental import pallas as pl
from jax.experimental.pallas import tpu as pltpu
from jax.sharding import PartitionSpec as P

MESH = pl.DeviceIdType.MESH
HD = 128
HEADS = 3
LEN = 256
FEAT = 384
ROWS = 768
COLS = 1152
WIDTH = 6144
NZ = 8
GROUPS = ((0, 1), (1, 2), (3, 2), (5, 2), (7, 1))
F32 = jnp.float32
BF16 = jnp.bfloat16


def kernel(
    doc_ref, hid_ref, wq_hbm, wo_hbm, out_ref,
    xin, wq, wo, turn, norm, mask, proj, res,
    xbuf, abuf, part, send3, recv3,
    load_sem, hand_sem, go_sem,
    t1s, t1r, t2s, s1s, s1r, a2s, a2r, b2s, b2r, a5s, a5r, b5s, b5r,
    s3s, s3r, wos, wor,
):
    s = lax.axis_index("section")
    t = lax.axis_index("tensor")
    z = lax.axis_index("dp")
    y, x = t // 4, t % 4
    first = s == 0

    def along_z(by):
        return (s, t, (z + by + NZ) % NZ)

    def in_plane(dy, dx):
        return (s, ((y + dy) % 4) * 4 + (x + dx) % 4, z)

    def copy(src, dst, send_sem, recv_sem, device):
        return pltpu.make_async_remote_copy(
            src_ref=src, dst_ref=dst, send_sem=send_sem, recv_sem=recv_sem,
            device_id=device, device_id_type=MESH,
        )

    load_q = pltpu.make_async_copy(wq_hbm.at[0], wq, load_sem.at[0])
    load_o = pltpu.make_async_copy(wo_hbm.at[0], wo.at[z], load_sem.at[1])
    load_x = pltpu.make_async_copy(hid_ref.at[0], xin, load_sem.at[2])

    @pl.when(s == 0)
    def _():
        load_x.start()

    load_q.start()
    load_o.start()

    barrier = pltpu.get_barrier_semaphore()

    def greet(device):
        pl.semaphore_signal(barrier, inc=1, device_id=device, device_id_type=MESH)

    def greet_plane(i, c):
        greet(in_plane(i // 4, i % 4))
        return c

    lax.fori_loop(1, 16, greet_plane, 0)

    def greet_line(i, c):
        greet(along_z(i))
        return c

    lax.fori_loop(1, NZ, greet_line, 0)

    @pl.when(s == 1)
    def _():
        def greet_before(i, c):
            greet((0, i, z))
            return c

        lax.fori_loop(0, 16, greet_before, 0)

    def hand():
        return copy(res, xin, hand_sem.at[0], hand_sem.at[1], (1, t, z))

    @pl.when(first)
    def _():
        load_x.wait()

    pl.semaphore_wait(barrier, jnp.where(first, 16, 0) + 15 + 7)

    def turn_copy(src, i, to):
        _, g, _ = in_plane(i // 4, i % 4)
        rows = pl.ds(pl.multiple_of(g * 16, 16), 16)
        cols = pl.ds(pl.multiple_of((t % 2) * FEAT, 128), FEAT)
        sems = t1s if to == 0 else t2s
        return copy(src.at[rows, :], turn.at[t // 2, :, cols], sems.at[i], t1r.at[i], (to, g, z))

    def turn_send(src, to):
        def body(i, c):
            turn_copy(src, i, to).start()
            return c

        lax.fori_loop(1 - to, 16, body, 0)

    def turn_drain(src, to):
        def body(i, c):
            turn_copy(src, i, to).wait_send()
            return c

        lax.fori_loop(1 - to, 16, body, 0)

    own_rows = pl.ds(pl.multiple_of(x * 16, 16), 16)

    def line_copy(k):
        by = (4, -3, 3, -2, 2, -1, 1)[k]
        device = along_z(by)
        return copy(norm.at[device[2]], xbuf.at[k, y, own_rows, :], s1s.at[k], s1r.at[k], device)

    def line_wait(k):
        there = xbuf.at[k, y, own_rows, :]
        pltpu.make_async_copy(there, there, s1r.at[k]).wait()

    def gather_copy(buf, sems, step, grp, h, j):
        k0, n = GROUPS[grp]
        own = pl.ds(pl.multiple_of(x * 16, 16), 16)
        cols = pl.ds(h * FEAT, FEAT)
        if step == 0:
            ref = buf.at[pl.ds(k0, n), y, own, cols]
        elif h == 0:
            ref = buf.at[pl.ds(k0, n), y, :, cols]
        else:
            ref = buf.at[pl.ds(k0, n), :, own, cols]
        device = in_plane(0, j) if (step == h) else in_plane(j, 0)
        return copy(ref, ref, sems[2 * step].at[grp, h, j - 1], sems[2 * step + 1].at[grp, h, j - 1], device)

    def gather_first(buf, sems, grp):
        k0, n = GROUPS[grp]
        for k in range(k0, min(k0 + n, 7)):
            line_wait(k)
        for h in range(2):
            for j in (2, 1, 3):
                gather_copy(buf, sems, 0, grp, h, j).start()

    def gather_second(buf, sems, grp):
        for h in range(2):
            for j in (1, 2, 3):
                gather_copy(buf, sems, 0, grp, h, j).wait_recv()
            for j in (2, 1, 3):
                gather_copy(buf, sems, 1, grp, h, j).start()

    def gather_last(buf, sems, grp):
        for h in range(2):
            for j in (1, 2, 3):
                gather_copy(buf, sems, 1, grp, h, j).wait_recv()

    def gather_drain(buf, sems):
        for grp in range(len(GROUPS)):
            for step in range(2):
                for h in range(2):
                    for j in (1, 2, 3):
                        gather_copy(buf, sems, step, grp, h, j).wait_send()

    @pl.when(first)
    def _():
        rows = pl.ds(pl.multiple_of(t * 16, 16), 16)
        turn[t // 2, :, pl.ds(pl.multiple_of((t % 2) * FEAT, 128), FEAT)] = xin[rows, :]
        turn_send(xin, 0)

    sems2 = (a2s, a2r, b2s, b2r)

    def weight_copy(step, way, part_of):
        chunk = (z + (step if way else -step) + NZ) % NZ
        near = way if part_of == 0 else 1 - way
        ref = wo.at[chunk, pl.ds(near * FEAT, FEAT)]
        return copy(ref, ref, wos.at[way, step, part_of], wor.at[way, step, part_of], along_z(-1 if way else 1))

    def weight_step(step):
        for part_of in range(2):
            for way in range(2):
                if step and (step, part_of) != (3, 1):
                    before = 2 if (step, part_of) == (4, 1) else step - 1
                    weight_copy(before, way, part_of).wait_recv()
                if step < 3 or (step == 3 and part_of == 0):
                    weight_copy(step, way, part_of).start()

    def weight_drain():
        for step in range(4):
            for way in range(2):
                weight_copy(step, way, 0).wait_send()
                if step < 3:
                    weight_copy(step, way, 1).wait_send()

    def product(buf, k, w, into, tiles):
        rows = buf[k].reshape(LEN, ROWS)

        def body(n, c):
            cols = pl.ds(pl.multiple_of(n * FEAT, 128), FEAT)
            into[k, :, cols] = jnp.dot(rows, w[:, cols], preferred_element_type=F32)
            return c

        lax.fori_loop(0, tiles, body, 0)

    def piece(c, r):
        return pl.ds(r * 128, 128), pl.ds(c * FEAT, FEAT)

    def ring_copy(k, c, r):
        rows, cols = piece(c, r)
        up = r == 0 if k == 0 else k % 2 == 1
        return copy(send3.at[k, rows, cols], recv3.at[k, rows, cols], s3s.at[k, c, r], s3r.at[k, c, r], along_z(1 if up else -1))

    def ring_step(k, c, r, before):
        rows, cols = piece(c, r)
        value = part[k, rows, cols]
        if before is not None:
            ring_copy(before, c, r).wait_recv()
            value = value + recv3[before, rows, cols].astype(F32)
        send3[k, rows, cols] = value.astype(BF16)
        ring_copy(k, c, r).start()

    @pl.when(s == 1)
    def _():
        pl.semaphore_wait(go_sem, 1)

    load_o.wait()
    weight_step(0)

    for i in range(1, 16):
        turn_copy(xin, i, 0).wait_recv()

    @pl.when(s == 1)
    def _():
        turn_copy(xin, 0, 0).wait_recv()

    whole = turn[...].astype(F32)
    mean = jnp.sum(jnp.sum(whole, axis=0), axis=1, keepdims=True) * (1.0 / WIDTH)
    off = whole - mean[None]
    spread = jnp.sum(jnp.sum(off * off, axis=0), axis=1, keepdims=True) * (1.0 / WIDTH)
    norm[...] = (off * lax.rsqrt(spread + 1e-05)[None]).astype(BF16)
    for k in range(7):
        line_copy(k).start()
    xbuf[7, y, own_rows, :] = norm[z]

    for grp in range(0, 5):
        gather_first(xbuf, sems2, grp)

    weight_step(1)

    row_pos = lax.broadcasted_iota(jnp.int32, (LEN, LEN), 0)
    col_pos = lax.broadcasted_iota(jnp.int32, (LEN, LEN), 1)
    row_doc = jnp.zeros((LEN, LEN), jnp.int32)
    col_doc = jnp.zeros((LEN, LEN), jnp.int32)
    end = jnp.int32(0)
    for i in range(4):
        end = end + doc_ref[0, i]
        row_doc = row_doc + (row_pos >= end).astype(jnp.int32)
        col_doc = col_doc + (col_pos >= end).astype(jnp.int32)
    mask[...] = jnp.where((col_pos <= row_pos) & (row_doc == col_doc), 1.0, 0.0)

    gather_second(xbuf, sems2, 0)
    gather_second(xbuf, sems2, 1)
    load_q.wait()
    gather_last(xbuf, sems2, 0)
    product(xbuf, 0, wq, part, 3)
    for c in range(3):
        ring_step(0, c, 0, None)
        ring_step(0, c, 1, None)
    gather_second(xbuf, sems2, 2)
    gather_last(xbuf, sems2, 1)
    product(xbuf, 1, wq, part, 3)
    for c in range(3):
        ring_step(1, c, 1, None)
    product(xbuf, 2, wq, part, 3)
    for c in range(3):
        ring_step(2, c, 0, None)
    gather_second(xbuf, sems2, 3)
    gather_last(xbuf, sems2, 2)
    product(xbuf, 3, wq, part, 3)
    product(xbuf, 4, wq, part, 3)
    for c in range(3):
        ring_step(1, c, 0, 0)
        ring_step(2, c, 1, 0)
    gather_second(xbuf, sems2, 4)
    gather_last(xbuf, sems2, 3)
    product(xbuf, 5, wq, part, 3)
    product(xbuf, 6, wq, part, 3)
    for c, r in ((0, 1), (1, 1), (0, 0), (2, 1), (1, 0), (2, 0)):
        ring_step(3, c, r, 1)
        ring_step(4, c, 1 - r, 2)
    gather_last(xbuf, sems2, 4)
    product(xbuf, 7, wq, part, 3)
    for c, r in ((0, 1), (0, 0), (1, 1), (1, 0), (2, 1), (2, 0)):
        ring_step(5, c, r, 3)
        ring_step(6, c, 1 - r, 4)

    weight_step(2)
    def head_copy(step, head, h, j):
        rows = pl.ds(h * 128, 128)
        own = pl.ds(pl.multiple_of((x % 2) * HD, 128), HD)
        if step == 0:
            ref = abuf.at[head, y, x // 2, rows, own]
        elif h == 0:
            ref = abuf.at[head, y, :, rows]
        else:
            ref = abuf.at[head, :, x // 2, rows, own]
        device = in_plane(0, j) if (step == h) else in_plane(j, 0)
        send, recv = (b5s, b5r) if step else (a5s, a5r)
        return copy(ref, ref, send.at[head, h, j - 1], recv.at[head, h, j - 1], device)

    allowed = mask[...] > 0.5
    for head in range(HEADS):
        base = head * 3 * HD
        for r in (1, 0):
            ring_copy(5, head, r).wait_recv()
            ring_copy(6, head, 1 - r).wait_recv()
        cols = pl.ds(base, FEAT)
        proj[:, cols] = (part[7, :, cols] + recv3[5, :, cols].astype(F32) + recv3[6, :, cols].astype(F32)).astype(BF16)
        query = proj[:, base : base + HD]
        keys = proj[:, base + HD : base + 2 * HD]
        values = proj[:, base + 2 * HD : base + 3 * HD]
        scores = lax.dot_general(query, keys, (((1,), (1,)), ((), ())), preferred_element_type=F32)
        scores = jnp.where(allowed, scores * (1.0 / math.sqrt(HD)), -1e30)
        weights = jnp.exp(scores - jnp.max(scores, axis=1, keepdims=True))
        soft = (weights / jnp.sum(weights, axis=1, keepdims=True)).astype(BF16)
        ahead = jnp.dot(soft, values, preferred_element_type=F32).astype(BF16)
        abuf[head, y, x // 2, :, pl.ds(pl.multiple_of((x % 2) * HD, 128), HD)] = ahead
        for h in range(2):
            for j in (2, 1, 3):
                head_copy(0, head, h, j).start()

    @pl.when(first)
    def _():
        turn_drain(xin, 0)

    for k in range(7):
        line_copy(k).wait_send()
    for head in range(HEADS):
        if head == HEADS - 1:
            weight_step(3)
        for h in range(2):
            for j in (1, 2, 3):
                head_copy(0, head, h, j).wait_recv()
            for j in (2, 1, 3):
                head_copy(1, head, h, j).start()

    gather_drain(xbuf, sems2)

    for k in range(7):
        for c in range(3):
            ring_copy(k, c, 0).wait_send()
            ring_copy(k, c, 1).wait_send()
    weight_step(4)

    @pl.when(first)
    def _():
        pl.semaphore_signal(go_sem, inc=1, device_id=(1, t, z), device_id_type=MESH)

    weight_drain()
    for head in range(HEADS):
        for h in range(2):
            for j in (1, 2, 3):
                head_copy(0, head, h, j).wait_send()

    @pl.when(s == 1)
    def _():
        hand().wait_recv()

    total = xin[...].astype(F32)
    for head in range(HEADS):
        for h in range(2):
            for j in (1, 2, 3):
                head_copy(1, head, h, j).wait_recv()
        for d in range(NZ):
            rows = jnp.concatenate([wo[d, head * HD : head * HD + HD], wo[d, FEAT + head * HD : FEAT + head * HD + HD]], axis=0)
            total = total + jnp.dot(abuf[head, d // 2, d % 2], rows, preferred_element_type=F32)
    result = total.astype(BF16)
    res[...] = result

    @pl.when(first)
    def _():
        turn_send(res, 1)
        hand().start()

    out_ref[0, 0] = res[...]
    for head in range(HEADS):
        for h in range(2):
            for j in (1, 2, 3):
                head_copy(1, head, h, j).wait_send()

    @pl.when(first)
    def _():
        turn_drain(res, 1)
        hand().wait_send()


def local(hidden_in, doc_lengths, w_qkv, w_out):
    vmem, dma = pltpu.VMEM, pltpu.SemaphoreType.DMA
    return pl.pallas_call(
        kernel,
        out_shape=jax.ShapeDtypeStruct((1, 1, LEN, FEAT), BF16),
        in_specs=[
            pl.BlockSpec(memory_space=pltpu.SMEM),
            pl.BlockSpec(memory_space=pl.ANY),
            pl.BlockSpec(memory_space=pl.ANY),
            pl.BlockSpec(memory_space=pl.ANY),
        ],
        out_specs=pl.BlockSpec(memory_space=pltpu.VMEM),
        scratch_shapes=[
            vmem((LEN, FEAT), BF16),
            vmem((ROWS, COLS), BF16),
            vmem((NZ, ROWS, FEAT), BF16),
            vmem((NZ, 16, ROWS), BF16),
            vmem((NZ, 16, ROWS), BF16),
            vmem((LEN, LEN), F32),
            vmem((LEN, COLS), BF16),
            vmem((LEN, FEAT), BF16),
            vmem((8, 4, 64, ROWS), BF16),
            vmem((HEADS, 4, 2, LEN, 2 * HD), BF16),
            vmem((8, LEN, COLS), F32),
            vmem((7, LEN, COLS), BF16),
            vmem((7, LEN, COLS), BF16),
            dma((3,)), dma((2,)), pltpu.SemaphoreType.REGULAR,
            dma((16,)), dma((16,)), dma((16,)), dma((7,)), dma((7,)),
            dma((5, 2, 3)), dma((5, 2, 3)), dma((5, 2, 3)), dma((5, 2, 3)),
            dma((3, 2, 3)), dma((3, 2, 3)), dma((3, 2, 3)), dma((3, 2, 3)),
            dma((7, 3, 2)), dma((7, 3, 2)), dma((2, 4, 2)), dma((2, 4, 2)),
        ],
        compiler_params=pltpu.CompilerParams(
            collective_id=0, has_side_effects=True, vmem_limit_bytes=56 * 1024 * 1024
        ),
        cost_estimate=pl.CostEstimate(
            flops=2 * 2048 * ROWS * (COLS + FEAT), bytes_accessed=3 * 1024 * 1024, transcendentals=3 * LEN * LEN
        ),
    )(doc_lengths, hidden_in, w_qkv, w_out)


def solution(mesh):
    return jax.shard_map(
        local,
        mesh=mesh,
        in_specs=(
            P("dp", None, "tensor"),
            P("dp", None),
            P("section", "dp", "tensor"),
            P("section", "dp", "tensor"),
        ),
        out_specs=P("section", "dp", None, "tensor"),
        check_vma=False,
    )
```

```python
import functools
import math

import jax
import jax.numpy as jnp
from jax import lax
from jax.experimental import pallas as pl
from jax.experimental.pallas import tpu as pltpu
from jax.sharding import PartitionSpec as P

MESH = pl.DeviceIdType.MESH
HD = 128
HEADS = 3
LEN = 256
FEAT = 384
ROWS = 768
COLS = 1152
WIDTH = 6144
NZ = 8
GROUPS = ((0, 1), (1, 2), (3, 2), (5, 2), (7, 1))
F32 = jnp.float32
BF16 = jnp.bfloat16


def kernel(
    doc_ref, hid_ref, wq_hbm, wo_hbm, out_ref,
    xin, wq, wo, turn, norm, mask, proj, res,
    xbuf, abuf, part, send3, recv3,
    load_sem, hand_sem, go_sem,
    t1s, t1r, t2s, s1s, s1r, a2s, a2r, b2s, b2r, a5s, a5r, b5s, b5r,
    s3s, s3r, wos, wor,
):
    s = lax.axis_index("section")
    t = lax.axis_index("tensor")
    z = lax.axis_index("dp")
    y, x = t // 4, t % 4
    first = s == 0

    def along_z(by):
        return (s, t, (z + by + NZ) % NZ)

    def in_plane(dy, dx):
        return (s, ((y + dy) % 4) * 4 + (x + dx) % 4, z)

    def copy(src, dst, send_sem, recv_sem, device):
        return pltpu.make_async_remote_copy(
            src_ref=src, dst_ref=dst, send_sem=send_sem, recv_sem=recv_sem,
            device_id=device, device_id_type=MESH,
        )

    load_q = pltpu.make_async_copy(wq_hbm.at[0], wq, load_sem.at[0])
    load_o = pltpu.make_async_copy(wo_hbm.at[0], wo.at[z], load_sem.at[1])
    load_x = pltpu.make_async_copy(hid_ref.at[0], xin, load_sem.at[2])

    @pl.when(s == 0)
    def _():
        load_x.start()

    load_q.start()
    load_o.start()

    barrier = pltpu.get_barrier_semaphore()

    def greet(device):
        pl.semaphore_signal(barrier, inc=1, device_id=device, device_id_type=MESH)

    def greet_plane(i, c):
        greet(in_plane(i // 4, i % 4))
        return c

    lax.fori_loop(1, 16, greet_plane, 0)

    def greet_line(i, c):
        greet(along_z(i))
        return c

    lax.fori_loop(1, NZ, greet_line, 0)

    @pl.when(s == 1)
    def _():
        def greet_before(i, c):
            greet((0, i, z))
            return c

        lax.fori_loop(0, 16, greet_before, 0)

    def hand():
        return copy(res, xin, hand_sem.at[0], hand_sem.at[1], (1, t, z))

    @pl.when(first)
    def _():
        load_x.wait()

    pl.semaphore_wait(barrier, jnp.where(first, 16, 0) + 15 + 7)

    def turn_copy(src, i, to):
        _, g, _ = in_plane(i // 4, i % 4)
        rows = pl.ds(pl.multiple_of(g * 16, 16), 16)
        cols = pl.ds(pl.multiple_of((t % 2) * FEAT, 128), FEAT)
        sems = t1s if to == 0 else t2s
        return copy(src.at[rows, :], turn.at[t // 2, :, cols], sems.at[i], t1r.at[i], (to, g, z))

    def turn_send(src, to):
        def body(i, c):
            turn_copy(src, i, to).start()
            return c

        lax.fori_loop(1 - to, 16, body, 0)

    def turn_drain(src, to):
        def body(i, c):
            turn_copy(src, i, to).wait_send()
            return c

        lax.fori_loop(1 - to, 16, body, 0)

    own_rows = pl.ds(pl.multiple_of(x * 16, 16), 16)

    def line_copy(k):
        by = (4, -3, 3, -2, 2, -1, 1)[k]
        device = along_z(by)
        return copy(norm.at[device[2]], xbuf.at[k, y, own_rows, :], s1s.at[k], s1r.at[k], device)

    def line_wait(k):
        there = xbuf.at[k, y, own_rows, :]
        pltpu.make_async_copy(there, there, s1r.at[k]).wait()

    def gather_copy(buf, sems, step, grp, h, j):
        k0, n = GROUPS[grp]
        own = pl.ds(pl.multiple_of(x * 16, 16), 16)
        cols = pl.ds(h * FEAT, FEAT)
        if step == 0:
            ref = buf.at[pl.ds(k0, n), y, own, cols]
        elif h == 0:
            ref = buf.at[pl.ds(k0, n), y, :, cols]
        else:
            ref = buf.at[pl.ds(k0, n), :, own, cols]
        device = in_plane(0, j) if (step == h) else in_plane(j, 0)
        return copy(ref, ref, sems[2 * step].at[grp, h, j - 1], sems[2 * step + 1].at[grp, h, j - 1], device)

    def gather_first(buf, sems, grp):
        k0, n = GROUPS[grp]
        for k in range(k0, min(k0 + n, 7)):
            line_wait(k)
        for h in range(2):
            for j in (2, 1, 3):
                gather_copy(buf, sems, 0, grp, h, j).start()

    def gather_second(buf, sems, grp):
        for h in range(2):
            for j in (1, 2, 3):
                gather_copy(buf, sems, 0, grp, h, j).wait_recv()
            for j in (2, 1, 3):
                gather_copy(buf, sems, 1, grp, h, j).start()

    def gather_last(buf, sems, grp):
        for h in range(2):
            for j in (1, 2, 3):
                gather_copy(buf, sems, 1, grp, h, j).wait_recv()

    def gather_drain(buf, sems):
        for grp in range(len(GROUPS)):
            for step in range(2):
                for h in range(2):
                    for j in (1, 2, 3):
                        gather_copy(buf, sems, step, grp, h, j).wait_send()

    @pl.when(first)
    def _():
        rows = pl.ds(pl.multiple_of(t * 16, 16), 16)
        turn[t // 2, :, pl.ds(pl.multiple_of((t % 2) * FEAT, 128), FEAT)] = xin[rows, :]
        turn_send(xin, 0)

    sems2 = (a2s, a2r, b2s, b2r)

    def weight_copy(step, way, part_of):
        chunk = (z + (step if way else -step) + NZ) % NZ
        near = way if part_of == 0 else 1 - way
        ref = wo.at[chunk, pl.ds(near * FEAT, FEAT)]
        return copy(ref, ref, wos.at[way, step, part_of], wor.at[way, step, part_of], along_z(-1 if way else 1))

    def weight_step(step):
        for part_of in range(2):
            for way in range(2):
                if step and (step, part_of) != (3, 1):
                    before = 2 if (step, part_of) == (4, 1) else step - 1
                    weight_copy(before, way, part_of).wait_recv()
                if step < 3 or (step == 3 and part_of == 0):
                    weight_copy(step, way, part_of).start()

    def weight_drain():
        for step in range(4):
            for way in range(2):
                weight_copy(step, way, 0).wait_send()
                if step < 3:
                    weight_copy(step, way, 1).wait_send()

    def product(buf, k, w, into, tiles):
        rows = buf[k].reshape(LEN, ROWS)

        def body(n, c):
            cols = pl.ds(pl.multiple_of(n * FEAT, 128), FEAT)
            into[k, :, cols] = jnp.dot(rows, w[:, cols], preferred_element_type=F32)
            return c

        lax.fori_loop(0, tiles, body, 0)

    def piece(c, r):
        return pl.ds(r * 128, 128), pl.ds(c * FEAT, FEAT)

    def ring_copy(k, c, r):
        rows, cols = piece(c, r)
        up = r == 0 if k == 0 else k % 2 == 1
        return copy(send3.at[k, rows, cols], recv3.at[k, rows, cols], s3s.at[k, c, r], s3r.at[k, c, r], along_z(1 if up else -1))

    def ring_step(k, c, r, before):
        rows, cols = piece(c, r)
        value = part[k, rows, cols]
        if before is not None:
            ring_copy(before, c, r).wait_recv()
            value = value + recv3[before, rows, cols].astype(F32)
        send3[k, rows, cols] = value.astype(BF16)
        ring_copy(k, c, r).start()

    @pl.when(s == 1)
    def _():
        pl.semaphore_wait(go_sem, 1)

    load_o.wait()
    weight_step(0)

    for i in range(1, 16):
        turn_copy(xin, i, 0).wait_recv()

    @pl.when(s == 1)
    def _():
        turn_copy(xin, 0, 0).wait_recv()

    whole = turn[...].astype(F32)
    mean = jnp.sum(jnp.sum(whole, axis=0), axis=1, keepdims=True) * (1.0 / WIDTH)
    off = whole - mean[None]
    spread = jnp.sum(jnp.sum(off * off, axis=0), axis=1, keepdims=True) * (1.0 / WIDTH)
    norm[...] = (off * lax.rsqrt(spread + 1e-05)[None]).astype(BF16)
    for k in range(7):
        line_copy(k).start()
    xbuf[7, y, own_rows, :] = norm[z]

    for grp in range(0, 5):
        gather_first(xbuf, sems2, grp)

    weight_step(1)

    row_pos = lax.broadcasted_iota(jnp.int32, (LEN, LEN), 0)
    col_pos = lax.broadcasted_iota(jnp.int32, (LEN, LEN), 1)
    row_doc = jnp.zeros((LEN, LEN), jnp.int32)
    col_doc = jnp.zeros((LEN, LEN), jnp.int32)
    end = jnp.int32(0)
    for i in range(4):
        end = end + doc_ref[0, i]
        row_doc = row_doc + (row_pos >= end).astype(jnp.int32)
        col_doc = col_doc + (col_pos >= end).astype(jnp.int32)
    mask[...] = jnp.where((col_pos <= row_pos) & (row_doc == col_doc), 1.0, 0.0)

    gather_second(xbuf, sems2, 0)
    gather_second(xbuf, sems2, 1)
    load_q.wait()
    gather_last(xbuf, sems2, 0)
    product(xbuf, 0, wq, part, 3)
    for c in range(3):
        ring_step(0, c, 0, None)
        ring_step(0, c, 1, None)
    gather_second(xbuf, sems2, 2)
    gather_last(xbuf, sems2, 1)
    product(xbuf, 1, wq, part, 3)
    for c in range(3):
        ring_step(1, c, 1, None)
    product(xbuf, 2, wq, part, 3)
    for c in range(3):
        ring_step(2, c, 0, None)
    gather_second(xbuf, sems2, 3)
    gather_last(xbuf, sems2, 2)
    product(xbuf, 3, wq, part, 3)
    product(xbuf, 4, wq, part, 3)
    for c in range(3):
        ring_step(1, c, 0, 0)
        ring_step(2, c, 1, 0)
    gather_second(xbuf, sems2, 4)
    for c, r in ((0, 1), (1, 1), (0, 0)):
        ring_step(3, c, r, 1)
        ring_step(4, c, 1 - r, 2)
    gather_last(xbuf, sems2, 3)
    product(xbuf, 5, wq, part, 3)
    product(xbuf, 6, wq, part, 3)
    for c, r in ((2, 1), (1, 0), (2, 0)):
        ring_step(3, c, r, 1)
        ring_step(4, c, 1 - r, 2)
    gather_last(xbuf, sems2, 4)
    product(xbuf, 7, wq, part, 3)
    for c, r in ((0, 1), (0, 0), (1, 1), (1, 0), (2, 1), (2, 0)):
        ring_step(5, c, r, 3)
        ring_step(6, c, 1 - r, 4)

    weight_step(2)
    def head_copy(step, head, h, j):
        rows = pl.ds(h * 128, 128)
        own = pl.ds(pl.multiple_of((x % 2) * HD, 128), HD)
        if step == 0:
            ref = abuf.at[head, y, x // 2, rows, own]
        elif h == 0:
            ref = abuf.at[head, y, :, rows]
        else:
            ref = abuf.at[head, :, x // 2, rows, own]
        device = in_plane(0, j) if (step == h) else in_plane(j, 0)
        send, recv = (b5s, b5r) if step else (a5s, a5r)
        return copy(ref, ref, send.at[head, h, j - 1], recv.at[head, h, j - 1], device)

    allowed = mask[...] > 0.5
    for head in range(HEADS):
        base = head * 3 * HD
        for r in (1, 0):
            ring_copy(5, head, r).wait_recv()
            ring_copy(6, head, 1 - r).wait_recv()
        cols = pl.ds(base, FEAT)
        proj[:, cols] = (part[7, :, cols] + recv3[5, :, cols].astype(F32) + recv3[6, :, cols].astype(F32)).astype(BF16)
        query = proj[:, base : base + HD]
        keys = proj[:, base + HD : base + 2 * HD]
        values = proj[:, base + 2 * HD : base + 3 * HD]
        scores = lax.dot_general(query, keys, (((1,), (1,)), ((), ())), preferred_element_type=F32)
        scores = jnp.where(allowed, scores * (1.0 / math.sqrt(HD)), -1e30)
        weights = jnp.exp(scores - jnp.max(scores, axis=1, keepdims=True))
        soft = (weights / jnp.sum(weights, axis=1, keepdims=True)).astype(BF16)
        ahead = jnp.dot(soft, values, preferred_element_type=F32).astype(BF16)
        abuf[head, y, x // 2, :, pl.ds(pl.multiple_of((x % 2) * HD, 128), HD)] = ahead
        for h in range(2):
            for j in (2, 1, 3):
                head_copy(0, head, h, j).start()

    @pl.when(first)
    def _():
        turn_drain(xin, 0)

    for k in range(7):
        line_copy(k).wait_send()
    for head in range(HEADS):
        if head == HEADS - 1:
            weight_step(3)
        for h in range(2):
            for j in (1, 2, 3):
                head_copy(0, head, h, j).wait_recv()
            for j in (2, 1, 3):
                head_copy(1, head, h, j).start()

    gather_drain(xbuf, sems2)

    for k in range(7):
        for c in range(3):
            ring_copy(k, c, 0).wait_send()
            ring_copy(k, c, 1).wait_send()
    weight_step(4)

    @pl.when(first)
    def _():
        pl.semaphore_signal(go_sem, inc=1, device_id=(1, t, z), device_id_type=MESH)

    weight_drain()
    for head in range(HEADS):
        for h in range(2):
            for j in (1, 2, 3):
                head_copy(0, head, h, j).wait_send()

    @pl.when(s == 1)
    def _():
        hand().wait_recv()

    total = xin[...].astype(F32)
    for head in range(HEADS):
        for h in range(2):
            for j in (1, 2, 3):
                head_copy(1, head, h, j).wait_recv()
        for d in range(NZ):
            rows = jnp.concatenate([wo[d, head * HD : head * HD + HD], wo[d, FEAT + head * HD : FEAT + head * HD + HD]], axis=0)
            total = total + jnp.dot(abuf[head, d // 2, d % 2], rows, preferred_element_type=F32)
    result = total.astype(BF16)
    res[...] = result

    @pl.when(first)
    def _():
        turn_send(res, 1)
        hand().start()

    out_ref[0, 0] = res[...]
    for head in range(HEADS):
        for h in range(2):
            for j in (1, 2, 3):
                head_copy(1, head, h, j).wait_send()

    @pl.when(first)
    def _():
        turn_drain(res, 1)
        hand().wait_send()


def local(hidden_in, doc_lengths, w_qkv, w_out):
    vmem, dma = pltpu.VMEM, pltpu.SemaphoreType.DMA
    return pl.pallas_call(
        kernel,
        out_shape=jax.ShapeDtypeStruct((1, 1, LEN, FEAT), BF16),
        in_specs=[
            pl.BlockSpec(memory_space=pltpu.SMEM),
            pl.BlockSpec(memory_space=pl.ANY),
            pl.BlockSpec(memory_space=pl.ANY),
            pl.BlockSpec(memory_space=pl.ANY),
        ],
        out_specs=pl.BlockSpec(memory_space=pltpu.VMEM),
        scratch_shapes=[
            vmem((LEN, FEAT), BF16),
            vmem((ROWS, COLS), BF16),
            vmem((NZ, ROWS, FEAT), BF16),
            vmem((NZ, 16, ROWS), BF16),
            vmem((NZ, 16, ROWS), BF16),
            vmem((LEN, LEN), F32),
            vmem((LEN, COLS), BF16),
            vmem((LEN, FEAT), BF16),
            vmem((8, 4, 64, ROWS), BF16),
            vmem((HEADS, 4, 2, LEN, 2 * HD), BF16),
            vmem((8, LEN, COLS), F32),
            vmem((7, LEN, COLS), BF16),
            vmem((7, LEN, COLS), BF16),
            dma((3,)), dma((2,)), pltpu.SemaphoreType.REGULAR,
            dma((16,)), dma((16,)), dma((16,)), dma((7,)), dma((7,)),
            dma((5, 2, 3)), dma((5, 2, 3)), dma((5, 2, 3)), dma((5, 2, 3)),
            dma((3, 2, 3)), dma((3, 2, 3)), dma((3, 2, 3)), dma((3, 2, 3)),
            dma((7, 3, 2)), dma((7, 3, 2)), dma((2, 4, 2)), dma((2, 4, 2)),
        ],
        compiler_params=pltpu.CompilerParams(
            collective_id=0, has_side_effects=True, vmem_limit_bytes=56 * 1024 * 1024
        ),
        cost_estimate=pl.CostEstimate(
            flops=2 * 2048 * ROWS * (COLS + FEAT), bytes_accessed=3 * 1024 * 1024, transcendentals=3 * LEN * LEN
        ),
    )(doc_lengths, hidden_in, w_qkv, w_out)


def solution(mesh):
    return jax.shard_map(
        local,
        mesh=mesh,
        in_specs=(
            P("dp", None, "tensor"),
            P("dp", None),
            P("section", "dp", "tensor"),
            P("section", "dp", "tensor"),
        ),
        out_specs=P("section", "dp", None, "tensor"),
        check_vma=False,
    )
```
